32 devices in a mesh: tm: 4 (over x, core), patch: 8 (over z, y).
Axes of the slice: x: 2, y: 2, z: 4, core: 2. Of those that a mesh axis runs over, the one named last changes fastest.
Arguments:
- stream: bfloat16 [4, 448, 1152], P('tm', 'patch'), may hold values from -6 to 6
- stale_keys: bfloat16 [4, 448, 1152], P(None, 'patch', 'tm'), may hold values from -10 to 10
- stale_values: bfloat16 [4, 448, 1152], P(None, 'patch', 'tm'), may hold values from -6 to 6
- modulation: float32 [2, 3, 1152], replicated, may hold values from -4 to 4
- w_qkv: bfloat16 [2, 3, 1152, 1152], P(None, None, 'tm'), may hold values from -0.1875 to 0.1875
- w_out: bfloat16 [2, 1152, 1152], P(None, 'tm'), may hold values from -0.1875 to 0.1875
- qk_gain: float32 [2, 2, 72], replicated, may hold values from 1.4 to 7
Outputs:
- output: bfloat16 [4, 448, 1152], P('tm', 'patch')
The draws below stay inside these ranges and needn't reach their ends.
All inputs are finite; a program needn't handle non-finite values.
Results may differ from the reference program's by a relative error of at most 0.035.
Values may be sent and summed in bfloat16 or wider, within the bound.
A program may use at most 64 MiB of HBM per device.

```python
import jax
import jax.numpy as jnp
from jax import lax

D = 1152
HEADS = 16
HEAD_DIM = 72
TOK_FRAME_DEV = 56
FRAMES = 4
SPATIAL = 448
N_TM = 4


def draw_qk_gain(key, part):
    key = jax.random.fold_in(key, 7)
    unit = jax.random.uniform(key, (2, 2, HEAD_DIM), jnp.float32)
    return 1.4 + 0.8 * unit


def block_levels(own_key, extent, split, least, largest):
    loudness, own = 1.0, jax.random.fold_in(own_key, 6)
    for dim, blocks in split:
        steps = jnp.exp(jax.random.uniform(jax.random.fold_in(own, dim), (blocks,), jnp.float32, least / len(split), largest / len(split)))
        loudness = loudness * jnp.repeat(steps, extent[dim] // blocks).reshape([-1 if axis == dim else 1 for axis in range(len(extent))])
    return loudness


def noise(key, shape, scale, limit, cuts=(), held_as=jnp.bfloat16):
    level = block_levels(key, shape, cuts, -0.22, 0.18) if cuts else 1.0
    array = jax.random.normal(key, shape, jnp.float32) * scale * level
    return jnp.minimum(jnp.maximum(array, -limit), limit).astype(held_as)


def setup_inputs(seed: int = 0) -> dict:
    streams_of = jax.random.split(jax.random.key(seed), 8)
    stream = noise(streams_of[0], (FRAMES, SPATIAL, D), 1.0, 6.0, ((0, 4), (1, 8)))
    stale_keys = noise(streams_of[1], (FRAMES, SPATIAL, D), 1.8, 10.0, ((1, 8), (2, 4)))
    stale_values = noise(streams_of[2], (FRAMES, SPATIAL, D), 1.0, 6.0, ((1, 8), (2, 4)))
    modulation = noise(streams_of[3], (2, 3, D), 0.7, 4.0, (), jnp.float32)
    w_qkv = noise(streams_of[4], (2, 3, D, D), D ** -0.5, 0.1875, ((2, 4),))
    w_out = noise(streams_of[5], (2, D, D), D ** -0.5, 0.1875, ((1, 4),))
    qk_gain = draw_qk_gain(jax.random.fold_in(streams_of[7], 71), 0)
    return {"stream": stream, "stale_keys": stale_keys, "stale_values": stale_values, "modulation": modulation, "w_qkv": w_qkv, "w_out": w_out, "qk_gain": qk_gain}


EPS = 1e-06

def softmax_rows(scores):
    top = lax.optimization_barrier(jnp.max(scores, axis=-1, keepdims=True))
    expo = jnp.exp(scores - top)
    return expo / lax.optimization_barrier(jnp.sum(expo, axis=-1, keepdims=True))

def modulate(stream, shift, scale):
    values = stream.astype(jnp.float32)
    center = lax.optimization_barrier(jnp.mean(values, axis=-1, keepdims=True))
    spread = lax.optimization_barrier(jnp.mean(jnp.square(values - center), axis=-1, keepdims=True))
    normed = (values - center) * lax.rsqrt(spread + EPS)
    return (normed * (1.0 + scale) + shift).astype(jnp.bfloat16)

def head_norm(values, gain):
    factor = lax.rsqrt(lax.optimization_barrier(jnp.mean(values * values, axis=-1, keepdims=True)) + EPS)
    return (values * factor * gain).astype(jnp.bfloat16)

def projections(stream, weights, gains, shift, scale):
    frames, spatial = (stream.shape[0], stream.shape[1])
    hmod = modulate(stream, shift, scale).reshape(frames * spatial, D)

    def one(matrix):
        raw = lax.dot_general(hmod, matrix, (((1,), (1,)), ((), ())), preferred_element_type=jnp.float32)
        return raw.reshape(frames, spatial, HEADS, HEAD_DIM)
    query = head_norm(one(weights[0]), gains[0])
    keys = head_norm(one(weights[1]), gains[1])
    values = one(weights[2]).astype(jnp.bfloat16)
    return (query, keys, values)

def spatial(query, keys, values, old_keys, old_values):
    block = jnp.arange(SPATIAL, dtype=jnp.int32) // TOK_FRAME_DEV
    same = (block[:, None] == block[None, :])[None]
    factor = HEAD_DIM ** (-0.5)

    def one(items):
        q, k, v, ok, ov = [a.astype(jnp.float32) for a in items]
        fresh = jnp.einsum('qhd,khd->hqk', q, k)
        older = jnp.einsum('qhd,khd->hqk', q, ok)
        scores = jnp.where(same, fresh, older) * factor
        weights = lax.optimization_barrier(softmax_rows(scores).astype(jnp.bfloat16)).astype(jnp.float32)
        near = jnp.einsum('hqk,khd->qhd', jnp.where(same, weights, jnp.float32(0.0)), v)
        far = jnp.einsum('hqk,khd->qhd', jnp.where(same, jnp.float32(0.0), weights), ov)
        return (near + far).astype(jnp.bfloat16)
    return lax.map(one, (query, keys, values, old_keys, old_values))

def temporal(query, keys, values):
    factor = HEAD_DIM ** (-0.5)
    scores = jnp.einsum('fshd,gshd->shfg', query.astype(jnp.float32), keys.astype(jnp.float32)) * factor
    weights = lax.optimization_barrier(softmax_rows(scores).astype(jnp.bfloat16)).astype(jnp.float32)
    return jnp.einsum('shfg,gshd->fshd', weights, values.astype(jnp.float32)).astype(jnp.bfloat16)

def out_sum(attn, matrix):
    width = D // N_TM

    def add(total, group):
        start = (group * width).astype(jnp.int32)
        piece = lax.dynamic_slice_in_dim(attn, start, width, 1)
        rows = lax.dynamic_slice_in_dim(matrix, start, width, 0)
        part = jnp.dot(piece, rows, preferred_element_type=jnp.float32).astype(jnp.bfloat16)
        return (total + part.astype(jnp.float32), None)
    total, _ = lax.scan(add, jnp.zeros((attn.shape[0], D), jnp.float32), jnp.arange(N_TM, dtype=jnp.int32))
    return total

def reference(stream, stale_keys, stale_values, modulation, w_qkv, w_out, qk_gain):
    frames, spatial_len = (stream.shape[0], stream.shape[1])
    shape4 = (frames, spatial_len, HEADS, HEAD_DIM)
    query, keys, values = projections(stream, w_qkv[0], qk_gain[0], modulation[0, 0], modulation[0, 1])
    attn = spatial(query, keys, values, stale_keys.reshape(shape4), stale_values.reshape(shape4))
    proj = out_sum(attn.reshape(frames * spatial_len, D), w_out[0]).reshape(frames, spatial_len, D)
    middle = (stream.astype(jnp.float32) + modulation[0, 2] * proj).astype(jnp.bfloat16)
    query, keys, values = projections(middle, w_qkv[1], qk_gain[1], modulation[1, 0], modulation[1, 1])
    attn = temporal(query, keys, values)
    proj = out_sum(attn.reshape(frames * spatial_len, D), w_out[1]).reshape(frames, spatial_len, D)
    return (middle.astype(jnp.float32) + modulation[1, 2] * proj).astype(jnp.bfloat16)
```

```python
import functools

import jax
import jax.numpy as jnp
from jax import lax
from jax.experimental import pallas as pl
from jax.experimental.pallas import tpu as pltpu
from jax.sharding import PartitionSpec as P

HEAD_DIM = 72
EPS = 1e-06
MESH = pl.DeviceIdType.MESH
F32 = jnp.float32
BF16 = jnp.bfloat16
NT = (((1,), (1,)), ((), ()))
NN = (((1,), (0,)), ((), ()))


def head_of(index, heads):
    total = jnp.zeros_like(index)
    for head in range(1, heads + 1):
        total = total + jnp.where(index >= head * HEAD_DIM, 1, 0)
    return total


def split_dot(left, right):
    high = left.astype(BF16)
    low = (left - high.astype(F32)).astype(BF16)
    return lax.dot_general(high, right, NN, preferred_element_type=F32) + lax.dot_general(
        low, right, NN, preferred_element_type=F32
    )


def kernel(
    n_tm, n_patch, width, wide,
    stream_ref, old_k_ref, old_v_ref, mod_ref, w_qkv_ref, w_out_ref, gain_ref,
    out_ref,
    wq, wo, own, buf, stage, acc, xg0, xg1, mid, hm, qbd, qkv, attn, part0, part1,
    rp0, rp1, sx0, sx1, rx0, rx1,
    w_sem, kv_send, kv_recv, ag_send_x, ag_send_p, ag_recv, rs_send_p, rs_recv_p, rs_send_x, rs_recv_x,
):
    frames, rows = old_k_ref.shape[0], old_k_ref.shape[1]
    depth = stream_ref.shape[2]
    heads = width // HEAD_DIM
    pad_rows = hm.shape[0] // frames
    held = w_out_ref.shape[1]
    packed = frames * width
    main = rows // 16 * 16
    tail = rows - main
    n_chip = n_tm // 2
    n_line = n_patch // 2
    scale = HEAD_DIM ** (-0.5)

    t = lax.axis_index("tm")
    chip, core = lax.div(t, 2), lax.rem(t, 2)
    partner = chip * 2 + 1 - core
    p = lax.axis_index("patch")
    a, b = lax.div(p, 2), lax.rem(p, 2)
    beside = a * 2 + 1 - b

    def other_chip(j):
        return lax.rem(chip + j, n_chip)

    loads = []
    for block in range(2):
        for c in range(3):
            loads.append(pltpu.make_async_copy(
                w_qkv_ref.at[block, c], wq.at[block, c, pl.ds(0, held)], w_sem.at[block * 4 + c]))
        loads.append(pltpu.make_async_copy(
            w_out_ref.at[block], wo.at[block, pl.ds(0, held)], w_sem.at[block * 4 + 3]))
    for load in loads:
        load.start()

    barrier = pltpu.get_barrier_semaphore()

    def greet(**where):
        pl.semaphore_signal(barrier, inc=1, device_id=where, device_id_type=MESH)

    greet(tm=partner)
    greet(patch=beside)
    for j in range(1, n_chip):
        greet(tm=other_chip(j) * 2 + core)

    @pl.when(a > 0)
    def _():
        greet(patch=p - 2)

    @pl.when(a < n_line - 1)
    def _():
        greet(patch=p + 2)

    met = 1 + n_chip + jnp.where(a > 0, 1, 0) + jnp.where(a < n_line - 1, 1, 0)
    pl.semaphore_wait(barrier, met)

    def remote(src, dst, send, recv, where):
        return pltpu.make_async_remote_copy(
            src_ref=src, dst_ref=dst, send_sem=send, recv_sem=recv, device_id=where, device_id_type=MESH)

    def gather_start(block, src, xg):
        sends = []
        for j in range(1, n_chip):
            sends.append(remote(src, xg.at[t], ag_send_x.at[block, j], ag_recv.at[block, t],
                                {"tm": other_chip(j) * 2 + core}))
        sends.append(remote(src, xg.at[t], ag_send_p.at[block, 0], ag_recv.at[block, t], {"tm": partner}))
        for send in sends:
            send.start()
        return sends

    def gather_arrived(block, xg, frame):
        remote(xg.at[frame], xg.at[frame], ag_send_p.at[block, 0], ag_recv.at[block, frame],
               {"tm": partner}).wait_recv()

    def gather_forward(block, xg):
        sends = []
        for j in range(1, n_chip):
            frame = other_chip(j) * 2 + core
            gather_arrived(block, xg, frame)
            send = remote(xg.at[frame], xg.at[frame], ag_send_p.at[block, j], ag_recv.at[block, frame],
                          {"tm": partner})
            send.start()
            sends.append(send)
        return sends

    def gather_finish(block, xg):
        for j in range(n_chip):
            gather_arrived(block, xg, other_chip(j) * 2 + 1 - core)

    pending = gather_start(0, stream_ref.at[0], xg0)
    xg0[t] = stream_ref[0]

    def window(frame):
        low = min(frame * width // 128 * 128, packed - wide)
        return low, frame * width - low

    def pack(slot):
        keys, values = acc[0], acc[1]
        slot[...] = jnp.concatenate(
            [keys[:main], values[:main], keys[main:], values[main:]], axis=0).astype(BF16)

    def place(which, frame, value):
        low, offset = window(frame)
        if offset:
            value = pltpu.roll(value, offset, 1)
        acc[which, :, low:low + wide] += value

    acc[...] = jnp.zeros_like(acc)
    stage[...] = jnp.zeros_like(stage)
    for frame in range(frames):
        for which, ref in enumerate((old_k_ref, old_v_ref)):
            stage[which, :, 0:width] = ref[frame].astype(F32)
            place(which, frame, stage[which])
    pack(own)

    def kv_copy(src, piece, kind, step, where):
        return remote(src, buf.at[piece], kv_send.at[kind, step], kv_recv.at[piece], {"patch": where})

    def relay(step, go):
        for kind, sign in ((0, 1), (1, -1)):
            origin = a - sign * step
            onward = a + sign
            piece = jnp.clip(origin, 0, n_line - 1) * 2 + b
            src = own if step == 0 else buf.at[piece]
            here = (origin >= 0) & (origin < n_line)

            @pl.when(here)
            def _():
                if step and go:
                    kv_copy(src, piece, kind, step, beside).wait_recv()
                if step:
                    across = kv_copy(src, piece, 2 + kind, step, beside)
                    across.start() if go else across.wait_send()

            @pl.when(here & (onward >= 0) & (onward < n_line))
            def _():
                along = kv_copy(src, piece, kind, step, jnp.clip(onward, 0, n_line - 1) * 2 + b)
                along.start() if go else along.wait_send()
        if step == 0:
            across = kv_copy(own, p, 2, 0, beside)
            across.start() if go else across.wait_send()

    relay(0, True)

    features = lax.broadcasted_iota(jnp.int32, (wide, wide), 0)
    columns = lax.broadcasted_iota(jnp.int32, (wide, wide), 1)
    same_head = (head_of(features, heads) == head_of(columns, heads)) & (features < width) & (columns < width)
    group = jnp.where(same_head, 1.0, 0.0).astype(BF16)
    lane = lax.broadcasted_iota(jnp.int32, (1, wide), 1)
    lane_head = head_of(lane, heads)
    down = lax.broadcasted_iota(jnp.int32, (HEAD_DIM, wide), 0)
    over = lax.broadcasted_iota(jnp.int32, (HEAD_DIM, wide), 1)
    over_head = head_of(over, heads)
    spread = jnp.where((over - HEAD_DIM * over_head == down) & (over_head < heads), 1.0, 0.0).astype(BF16)

    def gain_row(block, which):
        gain = gain_ref[block, which:which + 1, :]
        first = gain.astype(BF16)
        rest = gain - first.astype(F32)
        return lax.dot_general(first, spread, NN, preferred_element_type=F32) + split_dot(rest, spread)

    if wide > held:
        wq[:, :, held:, :] = jnp.zeros((2, 3, wide - held, depth), BF16)
        wo[:, held:, :] = jnp.zeros((2, wide - held, depth), BF16)

    def modulated(block, xg):
        shift, gain = mod_ref[block, 0:1], 1.0 + mod_ref[block, 1:2]
        for frame in range(frames):
            values = xg[frame].astype(F32)
            center = jnp.mean(values, axis=-1, keepdims=True)
            values = values - center
            spread_ = jnp.mean(values * values, axis=-1, keepdims=True)
            hmod = values * lax.rsqrt(spread_ + EPS) * gain + shift
            hmod = jnp.concatenate([hmod, jnp.zeros((pad_rows - rows, depth), F32)], axis=0)
            hm[frame * pad_rows:(frame + 1) * pad_rows, :] = hmod.astype(BF16)

    def projections(block):
        for c in range(3):
            loads[block * 4 + c].wait()
            raw = lax.dot_general(hm[...], wq[block, c], NT, preferred_element_type=F32)
            if c < 2:
                square = split_dot(raw * raw, group) * (1.0 / HEAD_DIM)
                raw = raw * lax.rsqrt(square + EPS) * gain_row(block, c)
            qkv[c] = raw

    def heads_out(block, part):
        loads[block * 4 + 3].wait()
        product = lax.dot_general(attn[...], wo[block], NN, preferred_element_type=F32)
        for frame in range(frames):
            part[frame] = product[frame * pad_rows:frame * pad_rows + rows].astype(BF16)

    def attn_store(frame, value):
        value = jnp.concatenate([value, jnp.zeros((pad_rows - rows, wide), F32)], axis=0)
        attn[frame * pad_rows:(frame + 1) * pad_rows, :] = value.astype(BF16)

    def reduced(block, part, rp, sx, rx):
        sends = []
        for j in list(range(1, n_chip)) + [0]:
            to = other_chip(j)
            send = remote(part.at[to * 2 + 1 - core], rp.at[to], rs_send_p.at[block, j], rs_recv_p.at[block, to],
                          {"tm": partner})
            send.start()
            sends.append(send)

        def arrived(to):
            remote(rp.at[to], rp.at[to], rs_send_p.at[block, 0], rs_recv_p.at[block, to],
                   {"tm": partner}).wait_recv()

        for j in range(1, n_chip):
            to = other_chip(j)
            arrived(to)
            sx[j - 1] = (part[to * 2 + core].astype(F32) + rp[to].astype(F32)).astype(BF16)
            send = remote(sx.at[j - 1], rx.at[j - 1], rs_send_x.at[block, j - 1], rs_recv_x.at[block, j - 1],
                          {"tm": to * 2 + core})
            send.start()
            sends.append(send)
        arrived(chip)
        total = part[t].astype(F32) + rp[chip].astype(F32)
        for j in range(1, n_chip):
            remote(sx.at[j - 1], rx.at[j - 1], rs_send_x.at[block, j - 1], rs_recv_x.at[block, j - 1],
                   {"tm": t}).wait_recv()
            total = total + rx[j - 1].astype(F32)
        return total, sends

    pending += gather_forward(0, xg0)
    gather_finish(0, xg0)
    modulated(0, xg0)
    if n_line > 1:
        relay(1, True)
    projections(0)
    acc[...] = jnp.zeros_like(acc)
    for frame in range(frames):
        start = frame * pad_rows
        for which in range(2):
            place(which, frame, qkv[1 + which, start:start + rows])
        _, offset = window(frame)
        query = qkv[0, start:start + rows]
        stacked = jnp.concatenate([jnp.where(lane_head == head, query, 0.0) for head in range(heads)], axis=0)
        if offset:
            stacked = pltpu.roll(stacked, offset, 1)
        qbd[frame] = stacked.astype(BF16)
    pack(buf.at[p])
    for step in range(2, n_line):
        relay(step, True)
    for line in range(n_line):
        piece = line * 2 + 1 - b
        kv_copy(own, piece, 2, 0, beside).wait_recv()

    spot = lax.broadcasted_iota(jnp.int32, (1, n_patch * 2 * tail), 1)
    real = (lax.rem(spot, 2 * tail) < tail)
    for frame in range(frames):
        low, offset = window(frame)
        keys = buf[:, 0:main, low:low + wide].reshape(n_patch * main, wide)
        values = buf[:, main:2 * main, low:low + wide].reshape(n_patch * main, wide)
        rest = buf[:, 2 * main:, low:low + wide].reshape(n_patch * 2 * tail, wide)
        query = qbd[frame]
        first = lax.dot_general(query, keys, NT, preferred_element_type=F32)
        second = lax.dot_general(query, rest, NT, preferred_element_type=F32)
        second = jnp.where(real, second, -1e30)
        top = jnp.maximum(jnp.max(first, axis=-1, keepdims=True), jnp.max(second, axis=-1, keepdims=True))
        first = jnp.exp((first - top) * scale)
        second = jnp.exp((second - top) * scale)
        norm = jnp.sum(first, axis=-1, keepdims=True) + jnp.sum(second, axis=-1, keepdims=True)
        second = pltpu.roll(second, tail, 1)
        mixed = lax.dot_general(first.astype(BF16), values, NN, preferred_element_type=F32)
        mixed = mixed + lax.dot_general(second.astype(BF16), rest, NN, preferred_element_type=F32)
        mixed = mixed / norm
        total = jnp.zeros((rows, wide), F32)
        for head in range(heads):
            start = offset + head * HEAD_DIM
            inside = (lane >= start) & (lane < start + HEAD_DIM)
            total = total + jnp.where(inside, mixed[head * rows:(head + 1) * rows], 0.0)
        if offset:
            total = pltpu.roll(total, wide - offset, 1)
        attn_store(frame, total)
    heads_out(0, part0)
    summed, sends = reduced(0, part0, rp0, sx0, rx0)
    pending += sends
    middle = (stream_ref[0].astype(F32) + mod_ref[0, 2:3] * summed).astype(BF16)
    mid[...] = middle
    pending += gather_start(1, mid, xg1)
    xg1[t] = middle

    pending += gather_forward(1, xg1)
    gather_finish(1, xg1)
    modulated(1, xg1)
    projections(1)
    for frame in range(frames):
        query = qkv[0, frame * pad_rows:frame * pad_rows + rows].astype(BF16).astype(F32)
        scores = []
        products = jnp.concatenate([
            query * qkv[1, g * pad_rows:g * pad_rows + rows].astype(BF16).astype(F32) for g in range(frames)], axis=0)
        products = split_dot(products, group) * scale
        scores = [products[g * rows:(g + 1) * rows] for g in range(frames)]
        top = functools.reduce(jnp.maximum, scores)
        scores = [jnp.exp(score - top) for score in scores]
        norm = 1.0 / functools.reduce(jnp.add, scores)
        total = jnp.zeros((rows, wide), F32)
        for g in range(frames):
            weight = (scores[g] * norm).astype(BF16).astype(F32)
            total = total + weight * qkv[2, g * pad_rows:g * pad_rows + rows].astype(BF16).astype(F32)
        attn_store(frame, total)
    heads_out(1, part1)
    summed, sends = reduced(1, part1, rp1, sx1, rx1)
    pending += sends
    out_ref[0] = (mid[...].astype(F32) + mod_ref[1, 2:3] * summed).astype(BF16)

    for send in pending:
        send.wait_send()
    for step in range(n_line):
        relay(step, False)


def local(n_tm, n_patch, stream, stale_keys, stale_values, modulation, w_qkv, w_out, qk_gain):
    frames, rows, width = stale_keys.shape
    depth = stream.shape[2]
    extra = -width % 16
    if extra:
        w_qkv = jnp.pad(w_qkv, ((0, 0), (0, 0), (0, extra), (0, 0)))
        w_out = jnp.pad(w_out, ((0, 0), (0, extra), (0, 0)))
    wide = max((frame * width % 128 + width + 127) // 128 * 128 for frame in range(frames))
    pad_rows = (rows + 15) // 16 * 16
    heads = width // HEAD_DIM
    n_chip, n_line = n_tm // 2, n_patch // 2
    vmem = pl.BlockSpec(memory_space=pltpu.VMEM)
    hbm = pl.BlockSpec(memory_space=pl.ANY)
    far = max(n_chip - 1, 1)
    return pl.pallas_call(
        functools.partial(kernel, n_tm, n_patch, width, wide),
        out_shape=jax.ShapeDtypeStruct(stream.shape, BF16),
        in_specs=[vmem, vmem, vmem, vmem, hbm, hbm, vmem],
        out_specs=vmem,
        scratch_shapes=[
            pltpu.VMEM((2, 3, wide, depth), BF16),
            pltpu.VMEM((2, wide, depth), BF16),
            pltpu.VMEM((2 * rows, frames * width), BF16),
            pltpu.VMEM((n_patch, 2 * rows, frames * width), BF16),
            pltpu.VMEM((2, rows, wide), F32),
            pltpu.VMEM((2, rows, frames * width), F32),
            pltpu.VMEM((frames, rows, depth), BF16),
            pltpu.VMEM((frames, rows, depth), BF16),
            pltpu.VMEM((rows, depth), BF16),
            pltpu.VMEM((frames * pad_rows, depth), BF16),
            pltpu.VMEM((frames, heads * rows, wide), BF16),
            pltpu.VMEM((3, frames * pad_rows, wide), F32),
            pltpu.VMEM((frames * pad_rows, wide), BF16),
            pltpu.VMEM((frames, rows, depth), BF16),
            pltpu.VMEM((frames, rows, depth), BF16),
            pltpu.VMEM((n_chip, rows, depth), BF16),
            pltpu.VMEM((n_chip, rows, depth), BF16),
            pltpu.VMEM((far, rows, depth), BF16),
            pltpu.VMEM((far, rows, depth), BF16),
            pltpu.VMEM((far, rows, depth), BF16),
            pltpu.VMEM((far, rows, depth), BF16),
            pltpu.SemaphoreType.DMA((8,)),
            pltpu.SemaphoreType.DMA((4, n_line)),
            pltpu.SemaphoreType.DMA((n_patch,)),
            pltpu.SemaphoreType.DMA((2, n_chip)),
            pltpu.SemaphoreType.DMA((2, n_chip)),
            pltpu.SemaphoreType.DMA((2, n_tm)),
            pltpu.SemaphoreType.DMA((2, n_chip)),
            pltpu.SemaphoreType.DMA((2, n_chip)),
            pltpu.SemaphoreType.DMA((2, far)),
            pltpu.SemaphoreType.DMA((2, far)),
        ],
        compiler_params=pltpu.CompilerParams(
            collective_id=0, has_side_effects=True, vmem_limit_bytes=48 * 1024 * 1024),
        cost_estimate=pl.CostEstimate(flops=4_000_000_000, bytes_accessed=8_000_000, transcendentals=1_000_000),
    )(stream, stale_keys, stale_values, modulation, w_qkv, w_out, qk_gain)


def solution(mesh):
    placed = (
        P("tm", "patch", None),
        P(None, "patch", "tm"),
        P(None, "patch", "tm"),
        P(),
        P(None, None, "tm", None),
        P(None, "tm", None),
        P(),
    )
    return jax.shard_map(
        functools.partial(local, mesh.shape["tm"], mesh.shape["patch"]),
        mesh=mesh, in_specs=placed, out_specs=P("tm", "patch", None), check_vma=False,
    )
```

```python
import functools

import jax
import jax.numpy as jnp
from jax import lax
from jax.experimental import pallas as pl
from jax.experimental.pallas import tpu as pltpu
from jax.sharding import PartitionSpec as P

HEAD_DIM = 72
EPS = 1e-06
MESH = pl.DeviceIdType.MESH
F32 = jnp.float32
BF16 = jnp.bfloat16
NT = (((1,), (1,)), ((), ()))
NN = (((1,), (0,)), ((), ()))


def head_of(index, heads):
    total = jnp.zeros_like(index)
    for head in range(1, heads + 1):
        total = total + jnp.where(index >= head * HEAD_DIM, 1, 0)
    return total


def split_dot(left, right):
    high = left.astype(BF16)
    low = (left - high.astype(F32)).astype(BF16)
    return lax.dot_general(high, right, NN, preferred_element_type=F32) + lax.dot_general(
        low, right, NN, preferred_element_type=F32
    )


def kernel(
    n_tm, n_patch, width, wide, parts,
    stream_ref, old_k_ref, old_v_ref, mod_ref, w_qkv_ref, w_out_ref, gain_ref,
    out_ref,
    wq, wo, old, mod, gains, own, buf, stage, acc, xg0, *rest_refs,
):
    n_part = len(parts)
    rest_refs = list(rest_refs)

    def take():
        return [rest_refs.pop(0) for _ in range(n_part)]

    xg1, mid, qbd = take(), take(), take()
    partial = [take(), take()]
    rp, sx, rx = [take(), take()], [take(), take()], [take(), take()]
    (w_sem, in_sem, kv_send, kv_recv, ag_send_x, ag_send_p, ag_recv,
     rs_send_p, rs_recv_p, rs_send_x, rs_recv_x) = rest_refs
    frames, rows = old_k_ref.shape[0], old_k_ref.shape[1]
    depth = stream_ref.shape[2]
    heads = width // HEAD_DIM
    held = w_out_ref.shape[1]
    packed = frames * width
    main = rows // 16 * 16
    tail = rows - main
    n_chip = n_tm // 2
    n_line = n_patch // 2
    scale = HEAD_DIM ** (-0.5)

    t = lax.axis_index("tm")
    chip, core = lax.div(t, 2), lax.rem(t, 2)
    partner = chip * 2 + 1 - core
    p = lax.axis_index("patch")
    a, b = lax.div(p, 2), lax.rem(p, 2)
    beside = a * 2 + 1 - b

    def other_chip(j):
        return lax.rem(chip + j, n_chip)

    inputs = [
        pltpu.make_async_copy(old_k_ref, old.at[0], in_sem.at[0]),
        pltpu.make_async_copy(old_v_ref, old.at[1], in_sem.at[1]),
        pltpu.make_async_copy(stream_ref.at[0], xg0.at[t], in_sem.at[2]),
        pltpu.make_async_copy(mod_ref, mod, in_sem.at[3]),
        pltpu.make_async_copy(gain_ref, gains, in_sem.at[4]),
    ]
    loads = []
    for block in range(2):
        for c in range(3):
            loads.append(pltpu.make_async_copy(
                w_qkv_ref.at[block, c], wq.at[block, c, pl.ds(0, held)], w_sem.at[block * 4 + c]))
        loads.append(pltpu.make_async_copy(
            w_out_ref.at[block], wo.at[block, pl.ds(0, held)], w_sem.at[block * 4 + 3]))
    for load in inputs + loads:
        load.start()

    barrier = pltpu.get_barrier_semaphore()

    def greet(**where):
        pl.semaphore_signal(barrier, inc=1, device_id=where, device_id_type=MESH)

    greet(tm=partner)
    greet(patch=beside)
    for j in range(1, n_chip):
        greet(tm=other_chip(j) * 2 + core)

    @pl.when(a > 0)
    def _():
        greet(patch=p - 2)

    @pl.when(a < n_line - 1)
    def _():
        greet(patch=p + 2)

    def window(frame):
        low = min(frame * width // 128 * 128, packed - wide)
        return low, frame * width - low

    def pack(slot):
        keys, values = acc[0], acc[1]
        slot[...] = jnp.concatenate(
            [keys[:main], values[:main], keys[main:], values[main:]], axis=0).astype(BF16)

    def place(which, frame, value):
        low, offset = window(frame)
        if offset:
            value = pltpu.roll(value, offset, 1)
        acc[which, :, low:low + wide] += value

    acc[...] = jnp.zeros_like(acc)
    stage[...] = jnp.zeros_like(stage)
    for which in range(2):
        inputs[which].wait()
        for frame in range(frames):
            stage[which, :, 0:width] = old[which, frame].astype(F32)
            place(which, frame, stage[which])
    pack(own)

    met = 1 + n_chip + jnp.where(a > 0, 1, 0) + jnp.where(a < n_line - 1, 1, 0)
    pl.semaphore_wait(barrier, met)

    def remote(src, dst, send, recv, where):
        return pltpu.make_async_remote_copy(
            src_ref=src, dst_ref=dst, send_sem=send, recv_sem=recv, device_id=where, device_id_type=MESH)

    pending = []

    def started(copy):
        copy.start()
        pending.append(copy)

    def kv_copy(src, piece, kind, step, where):
        return remote(src, buf.at[piece], kv_send.at[kind, step], kv_recv.at[piece], {"patch": where})

    def relay(step, go):
        for kind, sign in ((0, 1), (1, -1)):
            origin = a - sign * step
            onward = a + sign
            piece = jnp.clip(origin, 0, n_line - 1) * 2 + b
            src = own if step == 0 else buf.at[piece]
            here = (origin >= 0) & (origin < n_line)

            @pl.when(here)
            def _():
                if step and go:
                    kv_copy(src, piece, kind, step, beside).wait_recv()
                if step:
                    across = kv_copy(src, piece, 2 + kind, step, beside)
                    across.start() if go else across.wait_send()

            @pl.when(here & (onward >= 0) & (onward < n_line))
            def _():
                along = kv_copy(src, piece, kind, step, jnp.clip(onward, 0, n_line - 1) * 2 + b)
                along.start() if go else along.wait_send()
        if step == 0:
            across = kv_copy(own, p, 2, 0, beside)
            across.start() if go else across.wait_send()

    relay(0, True)

    def gather_start(phase, src, xg):
        for j in range(1, n_chip):
            started(remote(src, xg.at[t], ag_send_x.at[phase, j], ag_recv.at[phase, t],
                           {"tm": other_chip(j) * 2 + core}))
        started(remote(src, xg.at[t], ag_send_p.at[phase, 0], ag_recv.at[phase, t], {"tm": partner}))

    def gather_arrived(phase, xg, frame):
        remote(xg.at[frame], xg.at[frame], ag_send_p.at[phase, 0], ag_recv.at[phase, frame],
               {"tm": partner}).wait_recv()

    def gather_forward(phase, xg):
        for j in range(1, n_chip):
            frame = other_chip(j) * 2 + core
            gather_arrived(phase, xg, frame)
            started(remote(xg.at[frame], xg.at[frame], ag_send_p.at[phase, j], ag_recv.at[phase, frame],
                           {"tm": partner}))

    def gather_finish(phase, xg):
        for j in range(n_chip):
            gather_arrived(phase, xg, other_chip(j) * 2 + 1 - core)

    inputs[2].wait()
    gather_start(0, xg0.at[t], xg0)

    features = lax.broadcasted_iota(jnp.int32, (wide, wide), 0)
    columns = lax.broadcasted_iota(jnp.int32, (wide, wide), 1)
    same_head = (head_of(features, heads) == head_of(columns, heads)) & (features < width) & (columns < width)
    group = jnp.where(same_head, 1.0, 0.0).astype(BF16)
    lane = lax.broadcasted_iota(jnp.int32, (1, wide), 1)
    lane_head = head_of(lane, heads)
    down = lax.broadcasted_iota(jnp.int32, (HEAD_DIM, wide), 0)
    over = lax.broadcasted_iota(jnp.int32, (HEAD_DIM, wide), 1)
    over_head = head_of(over, heads)
    spread = jnp.where((over - HEAD_DIM * over_head == down) & (over_head < heads), 1.0, 0.0).astype(BF16)

    def gain_row(block, which):
        gain = gains[block, which:which + 1, :]
        first = gain.astype(BF16)
        rest = gain - first.astype(F32)
        return lax.dot_general(first, spread, NN, preferred_element_type=F32) + split_dot(rest, spread)

    if wide > held:
        wq[:, :, held:, :] = jnp.zeros((2, 3, wide - held, depth), BF16)
        wo[:, held:, :] = jnp.zeros((2, wide - held, depth), BF16)
    inputs[3].wait()
    inputs[4].wait()
    gain_rows = [[gain_row(block, c) for c in range(2)] for block in range(2)]

    def modulated(block, xg):
        shift, gain = mod[0, block:block + 1], 1.0 + mod[1, block:block + 1]
        out = []
        for frame in range(frames):
            values = xg[frame].astype(F32)
            center = jnp.mean(values, axis=-1, keepdims=True)
            values = values - center
            spread_ = jnp.mean(values * values, axis=-1, keepdims=True)
            out.append(values * lax.rsqrt(spread_ + EPS) * gain + shift)
        return jnp.concatenate(out, axis=0).astype(BF16)

    def projections(block, hmod):
        raw = lax.dot_general(
            hmod, wq[block].reshape(3 * wide, depth), NT, preferred_element_type=F32)
        out = []
        for c in range(2):
            piece = raw[:, c * wide:(c + 1) * wide]
            square = split_dot(piece * piece, group) * (1.0 / HEAD_DIM)
            out.append(piece * lax.rsqrt(square + EPS) * gain_rows[block][c])
        return out + [raw[:, 2 * wide:]]

    def heads_out(block, half, attn):
        count = parts[half][1]
        product = lax.dot_general(
            jnp.concatenate(attn, axis=0).astype(BF16), wo[block], NN, preferred_element_type=F32)
        for frame in range(frames):
            partial[block][half][frame] = product[frame * count:(frame + 1) * count].astype(BF16)

    def sum_start(block, half):
        phase = block * n_part + half
        part, inbox = partial[block][half], rp[block][half]
        for j in list(range(1, n_chip)) + [0]:
            to = other_chip(j)
            started(remote(part.at[to * 2 + 1 - core], inbox.at[to], rs_send_p.at[phase, j], rs_recv_p.at[phase, to],
                           {"tm": partner}))

    def sum_arrived(phase, inbox, to):
        remote(inbox.at[to], inbox.at[to], rs_send_p.at[phase, 0], rs_recv_p.at[phase, to],
               {"tm": partner}).wait_recv()

    def sum_across(block, half):
        phase = block * n_part + half
        part, inbox, outbox = partial[block][half], rp[block][half], sx[block][half]
        for j in range(1, n_chip):
            to = other_chip(j)
            sum_arrived(phase, inbox, to)
            outbox[j - 1] = (part[to * 2 + core].astype(F32) + inbox[to].astype(F32)).astype(BF16)
            started(remote(outbox.at[j - 1], rx[block][half].at[j - 1], rs_send_x.at[phase, j - 1],
                           rs_recv_x.at[phase, j - 1], {"tm": to * 2 + core}))

    def sum_finish(block, half):
        phase = block * n_part + half
        sum_arrived(phase, rp[block][half], chip)
        total = partial[block][half][t].astype(F32) + rp[block][half][chip].astype(F32)
        for j in range(1, n_chip):
            remote(sx[block][half].at[j - 1], rx[block][half].at[j - 1], rs_send_x.at[phase, j - 1],
                   rs_recv_x.at[phase, j - 1], {"tm": partner}).wait_recv()
            total = total + rx[block][half][j - 1].astype(F32)
        return total

    gather_forward(0, xg0)
    gather_finish(0, xg0)
    hmod = modulated(0, xg0)
    if n_line > 1:
        relay(1, True)
    for load in loads[:3]:
        load.wait()
    query, keys, values = projections(0, hmod)
    acc[...] = jnp.zeros_like(acc)
    for frame in range(frames):
        place(0, frame, keys[frame * rows:(frame + 1) * rows])
        place(1, frame, values[frame * rows:(frame + 1) * rows])
        _, offset = window(frame)
        for half, (first_row, count) in enumerate(parts):
            start = frame * rows + first_row
            some = query[start:start + count]
            some = jnp.concatenate([jnp.where(lane_head == head, some, 0.0) for head in range(heads)], axis=0)
            if offset:
                some = pltpu.roll(some, offset, 1)
            qbd[half][frame] = some.astype(BF16)
    pack(buf.at[p])
    for step in range(2, n_line):
        relay(step, True)
    for load in loads[3:]:
        load.wait()
    for line in range(n_line):
        piece = line * 2 + 1 - b
        kv_copy(own, piece, 2, 0, beside).wait_recv()

    spot = lax.broadcasted_iota(jnp.int32, (1, n_patch * 2 * tail), 1)
    real = (lax.rem(spot, 2 * tail) < tail)

    def spatial(frame, half):
        count = parts[half][1]
        low, offset = window(frame)
        keys = buf[:, 0:main, low:low + wide].reshape(n_patch * main, wide)
        values = buf[:, main:2 * main, low:low + wide].reshape(n_patch * main, wide)
        rest = buf[:, 2 * main:, low:low + wide].reshape(n_patch * 2 * tail, wide)
        query = qbd[half][frame]
        first = lax.dot_general(query, keys, NT, preferred_element_type=F32)
        second = lax.dot_general(query, rest, NT, preferred_element_type=F32)
        second = jnp.where(real, second, -1e30)
        top = jnp.maximum(jnp.max(first, axis=-1, keepdims=True), jnp.max(second, axis=-1, keepdims=True))
        first = jnp.exp((first - top) * scale)
        second = jnp.exp((second - top) * scale)
        norm = jnp.sum(first, axis=-1, keepdims=True) + jnp.sum(second, axis=-1, keepdims=True)
        second = pltpu.roll(second, tail, 1)
        mixed = lax.dot_general(first.astype(BF16), values, NN, preferred_element_type=F32)
        mixed = mixed + lax.dot_general(second.astype(BF16), rest, NN, preferred_element_type=F32)
        mixed = mixed / norm
        total = jnp.zeros((count, wide), F32)
        for head in range(heads):
            start = offset + head * HEAD_DIM
            inside = (lane >= start) & (lane < start + HEAD_DIM)
            total = total + jnp.where(inside, mixed[head * count:(head + 1) * count], 0.0)
        return pltpu.roll(total, wide - offset, 1) if offset else total

    def temporal(half, query, keys, values):
        count = parts[half][1]
        query, keys, values = [x.astype(BF16).astype(F32) for x in (query, keys, values)]
        out = []
        for frame in range(frames):
            one = query[frame * count:(frame + 1) * count]
            products = jnp.concatenate(
                [one * keys[g * count:(g + 1) * count] for g in range(frames)], axis=0)
            products = split_dot(products, group) * scale
            scores = [products[g * count:(g + 1) * count] for g in range(frames)]
            top = functools.reduce(jnp.maximum, scores)
            scores = [jnp.exp(score - top) for score in scores]
            norm = 1.0 / functools.reduce(jnp.add, scores)
            total = jnp.zeros((count, wide), F32)
            for g in range(frames):
                weight = (scores[g] * norm).astype(BF16).astype(F32)
                total = total + weight * values[g * count:(g + 1) * count]
            out.append(total)
        return out

    def middle(half):
        first_row, count = parts[half]
        summed = sum_finish(0, half)
        mine = xg0[t].astype(F32)[first_row:first_row + count]
        value = (mine + mod[2, 0:1] * summed).astype(BF16)
        mid[half][...] = value
        gather_start(1 + half, mid[half], xg1[half])
        xg1[half][t] = value

    def finish(half):
        return mid[half][...].astype(F32) + mod[2, 1:2] * sum_finish(1, half)

    for half in range(n_part):
        attn = []
        for frame in range(frames):
            attn.append(spatial(frame, half))
            if half and frame == frames // 2 - 1:
                sum_across(0, half - 1)
        heads_out(0, half, attn)
        sum_start(0, half)
    middle(0)
    sum_across(0, n_part - 1)
    gather_forward(1, xg1[0])
    for half in range(1, n_part):
        middle(half)
    for half in range(n_part):
        gather_finish(1 + half, xg1[half])
        hmod = modulated(1, xg1[half])
        if half + 1 < n_part:
            gather_forward(2 + half, xg1[half + 1])
        triple = projections(1, hmod)
        if half:
            sum_across(1, half - 1)
        heads_out(1, half, temporal(half, *triple))
        sum_start(1, half)
    sum_across(1, n_part - 1)
    result = [finish(half) for half in range(n_part)]
    out_ref[0] = jnp.concatenate(result, axis=0).astype(BF16)

    for copy in pending:
        copy.wait_send()
    for step in range(n_line):
        relay(step, False)


def local(n_tm, n_patch, stream, stale_keys, stale_values, modulation, w_qkv, w_out, qk_gain):
    frames, rows, width = stale_keys.shape
    depth = stream.shape[2]
    extra = -width % 16
    if extra:
        w_qkv = jnp.pad(w_qkv, ((0, 0), (0, 0), (0, extra), (0, 0)))
        w_out = jnp.pad(w_out, ((0, 0), (0, extra), (0, 0)))
    wide = max((frame * width % 128 + width + 127) // 128 * 128 for frame in range(frames))
    heads = width // HEAD_DIM
    n_chip, n_line = n_tm // 2, n_patch // 2
    cut = (rows // 2 + 15) // 16 * 16
    parts = ((0, cut), (cut, rows - cut))
    n_part = len(parts)
    vmem = pl.BlockSpec(memory_space=pltpu.VMEM)
    hbm = pl.BlockSpec(memory_space=pltpu.HBM)
    far = max(n_chip - 1, 1)

    def each(*lead):
        return [pltpu.VMEM((*lead, count, depth), BF16) for _, count in parts]

    dma = pltpu.SemaphoreType.DMA
    return pl.pallas_call(
        functools.partial(kernel, n_tm, n_patch, width, wide, parts),
        out_shape=jax.ShapeDtypeStruct(stream.shape, BF16),
        in_specs=[hbm] * 7,
        out_specs=vmem,
        scratch_shapes=[
            pltpu.VMEM((2, 3, wide, depth), BF16),
            pltpu.VMEM((2, wide, depth), BF16),
            pltpu.VMEM((2, frames, rows, width), BF16),
            pltpu.VMEM((3, 2, depth), F32),
            pltpu.VMEM((2, 2, HEAD_DIM), F32),
            pltpu.VMEM((2 * rows, frames * width), BF16),
            pltpu.VMEM((n_patch, 2 * rows, frames * width), BF16),
            pltpu.VMEM((2, rows, wide), F32),
            pltpu.VMEM((2, rows, frames * width), F32),
            pltpu.VMEM((frames, rows, depth), BF16),
            *each(frames),
            *each(),
            *[pltpu.VMEM((frames, heads * count, wide), BF16) for _, count in parts],
            *each(frames), *each(frames),
            *each(n_chip), *each(n_chip),
            *each(far), *each(far),
            *each(far), *each(far),
            dma((8,)),
            dma((5,)),
            dma((4, n_line)),
            dma((n_patch,)),
            dma((1 + n_part, n_chip)),
            dma((1 + n_part, n_chip)),
            dma((1 + n_part, n_tm)),
            dma((2 * n_part, n_chip)),
            dma((2 * n_part, n_chip)),
            dma((2 * n_part, far)),
            dma((2 * n_part, far)),
        ],
        compiler_params=pltpu.CompilerParams(
            collective_id=0, has_side_effects=True, vmem_limit_bytes=56 * 1024 * 1024),
        cost_estimate=pl.CostEstimate(flops=4_000_000_000, bytes_accessed=8_000_000, transcendentals=1_000_000),
    )(stream, stale_keys, stale_values, jnp.transpose(modulation, (1, 0, 2)), w_qkv, w_out, qk_gain)


def solution(mesh):
    placed = (
        P("tm", "patch", None),
        P(None, "patch", "tm"),
        P(None, "patch", "tm"),
        P(),
        P(None, None, "tm", None),
        P(None, "tm", None),
        P(),
    )
    return jax.shard_map(
        functools.partial(local, mesh.shape["tm"], mesh.shape["patch"]),
        mesh=mesh, in_specs=placed, out_specs=P("tm", "patch", None), check_vma=False,
    )
```

```python
import functools

import jax
import jax.numpy as jnp
from jax import lax
from jax.experimental import pallas as pl
from jax.experimental.pallas import tpu as pltpu
from jax.sharding import PartitionSpec as P

HEAD_DIM = 72
EPS = 1e-06
MESH = pl.DeviceIdType.MESH
F32 = jnp.float32
BF16 = jnp.bfloat16
NT = (((1,), (1,)), ((), ()))
NN = (((1,), (0,)), ((), ()))


def head_of(index, heads):
    total = jnp.zeros_like(index)
    for head in range(1, heads + 1):
        total = total + jnp.where(index >= head * HEAD_DIM, 1, 0)
    return total


def split_dot(left, right):
    high = left.astype(BF16)
    low = (left - high.astype(F32)).astype(BF16)
    return lax.dot_general(high, right, NN, preferred_element_type=F32) + lax.dot_general(
        low, right, NN, preferred_element_type=F32
    )


def kernel(
    n_tm, n_patch, width, wide, parts,
    stream_ref, old_k_ref, old_v_ref, mod_ref, w_qkv_ref, w_out_ref, gain_ref,
    out_ref,
    wq, wo, old, mod, gains, own, buf, stage, acc, xg0, *rest_refs,
):
    n_part = len(parts)
    rest_refs = list(rest_refs)

    def take():
        return [rest_refs.pop(0) for _ in range(n_part)]

    xg1, mid, qbd = take(), take(), take()
    partial = [take(), take()]
    rp, sx, rx = [take(), take()], [take(), take()], [take(), take()]
    (w_sem, in_sem, kv_send, kv_recv, ag_send_x, ag_send_p, ag_recv,
     rs_send_p, rs_recv_p, rs_send_x, rs_recv_x) = rest_refs
    frames, rows = old_k_ref.shape[0], old_k_ref.shape[1]
    depth = stream_ref.shape[2]
    heads = width // HEAD_DIM
    held = w_out_ref.shape[1]
    packed = frames * width
    main = rows // 16 * 16
    tail = rows - main
    n_chip = n_tm // 2
    n_line = n_patch // 2
    upper = rows // 16 * 16
    cuts = ((0, upper), (upper, 2 * rows - upper))
    scale = HEAD_DIM ** (-0.5)

    t = lax.axis_index("tm")
    chip, core = lax.div(t, 2), lax.rem(t, 2)
    partner = chip * 2 + 1 - core
    p = lax.axis_index("patch")
    a, b = lax.div(p, 2), lax.rem(p, 2)
    beside = a * 2 + 1 - b

    def other_chip(j):
        return lax.rem(chip + j, n_chip)

    inputs = [
        pltpu.make_async_copy(old_k_ref, old.at[0], in_sem.at[0]),
        pltpu.make_async_copy(old_v_ref, old.at[1], in_sem.at[1]),
        pltpu.make_async_copy(stream_ref.at[0], xg0.at[t], in_sem.at[2]),
        pltpu.make_async_copy(mod_ref, mod, in_sem.at[3]),
        pltpu.make_async_copy(gain_ref, gains, in_sem.at[4]),
    ]
    loads = []
    for block in range(2):
        for c in range(3):
            loads.append(pltpu.make_async_copy(
                w_qkv_ref.at[block, c], wq.at[block, c, pl.ds(0, held)], w_sem.at[block * 4 + c]))
        loads.append(pltpu.make_async_copy(
            w_out_ref.at[block], wo.at[block, pl.ds(0, held)], w_sem.at[block * 4 + 3]))
    for load in inputs + loads:
        load.start()

    barrier = pltpu.get_barrier_semaphore()

    def greet(**where):
        pl.semaphore_signal(barrier, inc=1, device_id=where, device_id_type=MESH)

    greet(tm=partner)
    greet(patch=beside)
    for j in range(1, n_chip):
        greet(tm=other_chip(j) * 2 + core)

    @pl.when(a > 0)
    def _():
        greet(patch=p - 2)

    @pl.when(a < n_line - 1)
    def _():
        greet(patch=p + 2)

    def window(frame):
        low = min(frame * width // 128 * 128, packed - wide)
        return low, frame * width - low

    def pack(slot):
        keys, values = acc[0], acc[1]
        slot[...] = jnp.concatenate(
            [keys[:main], values[:main], keys[main:], values[main:]], axis=0).astype(BF16)

    def place(which, frame, value):
        low, offset = window(frame)
        if offset:
            value = pltpu.roll(value, offset, 1)
        acc[which, :, low:low + wide] += value

    acc[...] = jnp.zeros_like(acc)
    stage[...] = jnp.zeros_like(stage)
    for which in range(2):
        inputs[which].wait()
        for frame in range(frames):
            stage[which, :, 0:width] = old[which, frame].astype(F32)
            place(which, frame, stage[which])
    pack(own)

    met = 1 + n_chip + jnp.where(a > 0, 1, 0) + jnp.where(a < n_line - 1, 1, 0)
    pl.semaphore_wait(barrier, met)

    def remote(src, dst, send, recv, where):
        return pltpu.make_async_remote_copy(
            src_ref=src, dst_ref=dst, send_sem=send, recv_sem=recv, device_id=where, device_id_type=MESH)

    pending = []

    def started(copy):
        copy.start()
        pending.append(copy)

    def kv_copy(src, line, side, cut, kind, step, **where):
        first, count = cuts[cut]
        rows_of = pl.ds(first, count)
        return remote(src.at[rows_of], buf.at[side, line, rows_of], kv_send.at[kind, step, cut],
                      kv_recv.at[side, line, cut], where)

    def kv_arrived(line, side, cut):
        kv_copy(own, line, side, cut, 0, 0, patch=beside).wait_recv()

    def move(copy, go):
        copy.start() if go else copy.wait_send()

    def spot_on_line(line):
        return jnp.clip(line, 0, n_line - 1)

    even = n_line == 4
    at_end = (a == 0) | (a == n_line - 1)
    inward = jnp.where(a == 0, 1, a - 1)
    outward = jnp.where(a == 1, 0, n_line - 1)
    far_end = jnp.where(a == 1, n_line - 1, 0)

    def relay(step, cut, go):
        for kind, sign in ((0, 1), (1, -1)):
            origin = a - sign * step
            onward = a + sign
            line = spot_on_line(origin)
            src = buf.at[b, line] if step else own
            here = (origin >= 0) & (origin < n_line)

            if step:
                @pl.when(here)
                def _():
                    if go:
                        kv_arrived(line, b, cut)

                across = here
                if even and step == 1:
                    across = here & (origin != 0) & (origin != n_line - 1)
                if even and step == n_line - 1 and cut == 1:
                    across = None
                if across is not None:
                    @pl.when(across)
                    def _():
                        move(kv_copy(src, line, b, cut, 2 + kind, step, patch=beside), go)

            @pl.when(here & (onward >= 0) & (onward < n_line))
            def _():
                move(kv_copy(src, line, b, cut, kind, step, patch=spot_on_line(onward) * 2 + b), go)
        if step == 0:
            move(kv_copy(own, a, b, cut, 2, 0, patch=beside), go)

    def relay_end(cut, go):
        if even:
            @pl.when(at_end)
            def _():
                if go:
                    kv_arrived(a, 1 - b, cut)
                move(kv_copy(buf.at[1 - b, a], a, 1 - b, cut, 4, 0, patch=inward * 2 + b), go)

    def relay_far(go):
        if even:
            @pl.when(jnp.logical_not(at_end))
            def _():
                if go:
                    kv_arrived(far_end, 1 - b, 1)
                move(kv_copy(buf.at[1 - b, far_end], far_end, 1 - b, 1, 4, 1, patch=outward * 2 + b), go)

    def final_waits():
        for line in range(n_line):
            for cut in range(2):
                forwarded = False
                if even and line in (0, n_line - 1):
                    forwarded = at_end & (a == line)
                    if cut == 1:
                        forwarded = forwarded | (jnp.logical_not(at_end) & (far_end == line))

                if forwarded is False:
                    kv_arrived(line, 1 - b, cut)
                else:
                    @pl.when(jnp.logical_not(forwarded))
                    def _():
                        kv_arrived(line, 1 - b, cut)

    for cut in range(2):
        relay(0, cut, True)

    def gather_start(phase, src, xg):
        for j in range(1, n_chip):
            started(remote(src, xg.at[t], ag_send_x.at[phase, j], ag_recv.at[phase, t],
                           {"tm": other_chip(j) * 2 + core}))
        started(remote(src, xg.at[t], ag_send_p.at[phase, 0], ag_recv.at[phase, t], {"tm": partner}))

    def gather_arrived(phase, xg, frame):
        remote(xg.at[frame], xg.at[frame], ag_send_p.at[phase, 0], ag_recv.at[phase, frame],
               {"tm": partner}).wait_recv()

    def gather_forward(phase, xg):
        for j in range(1, n_chip):
            frame = other_chip(j) * 2 + core
            gather_arrived(phase, xg, frame)
            started(remote(xg.at[frame], xg.at[frame], ag_send_p.at[phase, j], ag_recv.at[phase, frame],
                           {"tm": partner}))

    def gather_finish(phase, xg):
        for j in range(n_chip):
            gather_arrived(phase, xg, other_chip(j) * 2 + 1 - core)

    inputs[2].wait()
    gather_start(0, xg0.at[t], xg0)

    features = lax.broadcasted_iota(jnp.int32, (wide, wide), 0)
    columns = lax.broadcasted_iota(jnp.int32, (wide, wide), 1)
    same_head = (head_of(features, heads) == head_of(columns, heads)) & (features < width) & (columns < width)
    group = jnp.where(same_head, 1.0, 0.0).astype(BF16)
    lane = lax.broadcasted_iota(jnp.int32, (1, wide), 1)
    lane_head = head_of(lane, heads)
    down = lax.broadcasted_iota(jnp.int32, (HEAD_DIM, wide), 0)
    over = lax.broadcasted_iota(jnp.int32, (HEAD_DIM, wide), 1)
    over_head = head_of(over, heads)
    spread = jnp.where((over - HEAD_DIM * over_head == down) & (over_head < heads), 1.0, 0.0).astype(BF16)

    def gain_row(block, which):
        gain = gains[block, which:which + 1, :]
        first = gain.astype(BF16)
        rest = gain - first.astype(F32)
        return lax.dot_general(first, spread, NN, preferred_element_type=F32) + split_dot(rest, spread)

    if wide > held:
        wq[:, :, held:, :] = jnp.zeros((2, 3, wide - held, depth), BF16)
        wo[:, held:, :] = jnp.zeros((2, wide - held, depth), BF16)
    inputs[3].wait()
    inputs[4].wait()
    gain_rows = [[gain_row(block, c) for c in range(2)] for block in range(2)]

    def modulated(block, xg):
        shift, gain = mod[0, block:block + 1], 1.0 + mod[1, block:block + 1]
        out = []
        for frame in range(frames):
            values = xg[frame].astype(F32)
            center = jnp.mean(values, axis=-1, keepdims=True)
            values = values - center
            spread_ = jnp.mean(values * values, axis=-1, keepdims=True)
            out.append(values * lax.rsqrt(spread_ + EPS) * gain + shift)
        return jnp.concatenate(out, axis=0).astype(BF16)

    def projections(block, hmod):
        raw = lax.dot_general(
            hmod, wq[block].reshape(3 * wide, depth), NT, preferred_element_type=F32)
        out = []
        for c in range(2):
            piece = raw[:, c * wide:(c + 1) * wide]
            square = split_dot(piece * piece, group) * (1.0 / HEAD_DIM)
            out.append(piece * lax.rsqrt(square + EPS) * gain_rows[block][c])
        return out + [raw[:, 2 * wide:]]

    def heads_out(block, half, attn):
        count = parts[half][1]
        product = lax.dot_general(
            jnp.concatenate(attn, axis=0).astype(BF16), wo[block], NN, preferred_element_type=F32)
        for frame in range(frames):
            partial[block][half][frame] = product[frame * count:(frame + 1) * count].astype(BF16)

    def sum_start(block, half):
        phase = block * n_part + half
        part, inbox = partial[block][half], rp[block][half]
        for j in list(range(1, n_chip)) + [0]:
            to = other_chip(j)
            started(remote(part.at[to * 2 + 1 - core], inbox.at[to], rs_send_p.at[phase, j], rs_recv_p.at[phase, to],
                           {"tm": partner}))

    def sum_arrived(phase, inbox, to):
        remote(inbox.at[to], inbox.at[to], rs_send_p.at[phase, 0], rs_recv_p.at[phase, to],
               {"tm": partner}).wait_recv()

    def sum_across(block, half):
        phase = block * n_part + half
        part, inbox, outbox = partial[block][half], rp[block][half], sx[block][half]
        for j in range(1, n_chip):
            to = other_chip(j)
            sum_arrived(phase, inbox, to)
            outbox[j - 1] = (part[to * 2 + core].astype(F32) + inbox[to].astype(F32)).astype(BF16)
            started(remote(outbox.at[j - 1], rx[block][half].at[j - 1], rs_send_x.at[phase, j - 1],
                           rs_recv_x.at[phase, j - 1], {"tm": to * 2 + core}))

    def sum_finish(block, half):
        phase = block * n_part + half
        sum_arrived(phase, rp[block][half], chip)
        total = partial[block][half][t].astype(F32) + rp[block][half][chip].astype(F32)
        for j in range(1, n_chip):
            remote(sx[block][half].at[j - 1], rx[block][half].at[j - 1], rs_send_x.at[phase, j - 1],
                   rs_recv_x.at[phase, j - 1], {"tm": partner}).wait_recv()
            total = total + rx[block][half][j - 1].astype(F32)
        return total

    gather_forward(0, xg0)
    if n_line > 1:
        relay(1, 0, True)
        relay_end(0, True)
    gather_finish(0, xg0)
    hmod = modulated(0, xg0)
    if n_line > 1:
        relay(1, 1, True)
        relay_end(1, True)
    for load in loads[:3]:
        load.wait()
    query, keys, values = projections(0, hmod)
    if n_line > 2:
        relay(2, 0, True)
    acc[...] = jnp.zeros_like(acc)
    for frame in range(frames):
        place(0, frame, keys[frame * rows:(frame + 1) * rows])
        place(1, frame, values[frame * rows:(frame + 1) * rows])
        _, offset = window(frame)
        for half, (first_row, count) in enumerate(parts):
            start = frame * rows + first_row
            some = query[start:start + count]
            some = jnp.concatenate([jnp.where(lane_head == head, some, 0.0) for head in range(heads)], axis=0)
            if offset:
                some = pltpu.roll(some, offset, 1)
            qbd[half][frame] = some.astype(BF16)
    pack(buf.at[b, a])
    for step in range(2, n_line):
        for cut in range(2):
            if (step, cut) != (2, 0):
                relay(step, cut, True)
    relay_far(True)
    for load in loads[3:]:
        load.wait()
    final_waits()

    spot = lax.broadcasted_iota(jnp.int32, (1, n_patch * 2 * tail), 1)
    real = (lax.rem(spot, 2 * tail) < tail)

    def spatial(frame, half):
        count = parts[half][1]
        low, offset = window(frame)
        keys = buf[:, :, 0:main, low:low + wide].reshape(n_patch * main, wide)
        values = buf[:, :, main:2 * main, low:low + wide].reshape(n_patch * main, wide)
        rest = buf[:, :, 2 * main:, low:low + wide].reshape(n_patch * 2 * tail, wide)
        query = qbd[half][frame]
        first = lax.dot_general(query, keys, NT, preferred_element_type=F32)
        second = lax.dot_general(query, rest, NT, preferred_element_type=F32)
        second = jnp.where(real, second, -1e30)
        top = jnp.maximum(jnp.max(first, axis=-1, keepdims=True), jnp.max(second, axis=-1, keepdims=True))
        first = jnp.exp((first - top) * scale)
        second = jnp.exp((second - top) * scale)
        norm = jnp.sum(first, axis=-1, keepdims=True) + jnp.sum(second, axis=-1, keepdims=True)
        second = pltpu.roll(second, tail, 1)
        mixed = lax.dot_general(first.astype(BF16), values, NN, preferred_element_type=F32)
        mixed = mixed + lax.dot_general(second.astype(BF16), rest, NN, preferred_element_type=F32)
        mixed = mixed / norm
        total = jnp.zeros((count, wide), F32)
        for head in range(heads):
            start = offset + head * HEAD_DIM
            inside = (lane >= start) & (lane < start + HEAD_DIM)
            total = total + jnp.where(inside, mixed[head * count:(head + 1) * count], 0.0)
        return pltpu.roll(total, wide - offset, 1) if offset else total

    def temporal(half, query, keys, values):
        count = parts[half][1]
        query, keys, values = [x.astype(BF16).astype(F32) for x in (query, keys, values)]
        out = []
        for frame in range(frames):
            one = query[frame * count:(frame + 1) * count]
            products = jnp.concatenate(
                [one * keys[g * count:(g + 1) * count] for g in range(frames)], axis=0)
            products = split_dot(products, group) * scale
            scores = [products[g * count:(g + 1) * count] for g in range(frames)]
            top = functools.reduce(jnp.maximum, scores)
            scores = [jnp.exp(score - top) for score in scores]
            norm = 1.0 / functools.reduce(jnp.add, scores)
            total = jnp.zeros((count, wide), F32)
            for g in range(frames):
                weight = (scores[g] * norm).astype(BF16).astype(F32)
                total = total + weight * values[g * count:(g + 1) * count]
            out.append(total)
        return out

    def middle(half):
        first_row, count = parts[half]
        summed = sum_finish(0, half)
        mine = xg0[t].astype(F32)[first_row:first_row + count]
        value = (mine + mod[2, 0:1] * summed).astype(BF16)
        mid[half][...] = value
        gather_start(1 + half, mid[half], xg1[half])
        xg1[half][t] = value

    def finish(half):
        return mid[half][...].astype(F32) + mod[2, 1:2] * sum_finish(1, half)

    for half in range(n_part):
        attn = []
        for frame in range(frames):
            attn.append(spatial(frame, half))
            if half and frame == frames // 2 - 1:
                sum_across(0, half - 1)
        heads_out(0, half, attn)
        sum_start(0, half)
    middle(0)
    sum_across(0, n_part - 1)
    gather_forward(1, xg1[0])
    for half in range(1, n_part):
        middle(half)
    for half in range(n_part):
        gather_finish(1 + half, xg1[half])
        hmod = modulated(1, xg1[half])
        if half + 1 < n_part:
            gather_forward(2 + half, xg1[half + 1])
        triple = projections(1, hmod)
        if half:
            sum_across(1, half - 1)
        heads_out(1, half, temporal(half, *triple))
        sum_start(1, half)
    sum_across(1, n_part - 1)
    result = [finish(half) for half in range(n_part)]
    out_ref[0] = jnp.concatenate(result, axis=0).astype(BF16)

    for copy in pending:
        copy.wait_send()
    for step in range(n_line):
        for cut in range(2):
            relay(step, cut, False)
    for cut in range(2):
        relay_end(cut, False)
    relay_far(False)


def local(n_tm, n_patch, stream, stale_keys, stale_values, modulation, w_qkv, w_out, qk_gain):
    frames, rows, width = stale_keys.shape
    depth = stream.shape[2]
    extra = -width % 16
    if extra:
        w_qkv = jnp.pad(w_qkv, ((0, 0), (0, 0), (0, extra), (0, 0)))
        w_out = jnp.pad(w_out, ((0, 0), (0, extra), (0, 0)))
    wide = max((frame * width % 128 + width + 127) // 128 * 128 for frame in range(frames))
    heads = width // HEAD_DIM
    n_chip, n_line = n_tm // 2, n_patch // 2
    cut = (rows // 2 + 15) // 16 * 16
    parts = ((0, cut), (cut, rows - cut))
    n_part = len(parts)
    vmem = pl.BlockSpec(memory_space=pltpu.VMEM)
    hbm = pl.BlockSpec(memory_space=pltpu.HBM)
    far = max(n_chip - 1, 1)

    def each(*lead):
        return [pltpu.VMEM((*lead, count, depth), BF16) for _, count in parts]

    dma = pltpu.SemaphoreType.DMA
    return pl.pallas_call(
        functools.partial(kernel, n_tm, n_patch, width, wide, parts),
        out_shape=jax.ShapeDtypeStruct(stream.shape, BF16),
        in_specs=[hbm] * 7,
        out_specs=vmem,
        scratch_shapes=[
            pltpu.VMEM((2, 3, wide, depth), BF16),
            pltpu.VMEM((2, wide, depth), BF16),
            pltpu.VMEM((2, frames, rows, width), BF16),
            pltpu.VMEM((3, 2, depth), F32),
            pltpu.VMEM((2, 2, HEAD_DIM), F32),
            pltpu.VMEM((2 * rows, frames * width), BF16),
            pltpu.VMEM((2, n_line, 2 * rows, frames * width), BF16),
            pltpu.VMEM((2, rows, wide), F32),
            pltpu.VMEM((2, rows, frames * width), F32),
            pltpu.VMEM((frames, rows, depth), BF16),
            *each(frames),
            *each(),
            *[pltpu.VMEM((frames, heads * count, wide), BF16) for _, count in parts],
            *each(frames), *each(frames),
            *each(n_chip), *each(n_chip),
            *each(far), *each(far),
            *each(far), *each(far),
            dma((8,)),
            dma((5,)),
            dma((5, max(n_line, 2), 2)),
            dma((2, n_line, 2)),
            dma((1 + n_part, n_chip)),
            dma((1 + n_part, n_chip)),
            dma((1 + n_part, n_tm)),
            dma((2 * n_part, n_chip)),
            dma((2 * n_part, n_chip)),
            dma((2 * n_part, far)),
            dma((2 * n_part, far)),
        ],
        compiler_params=pltpu.CompilerParams(
            collective_id=0, has_side_effects=True, vmem_limit_bytes=56 * 1024 * 1024),
        cost_estimate=pl.CostEstimate(flops=4_000_000_000, bytes_accessed=8_000_000, transcendentals=1_000_000),
    )(stream, stale_keys, stale_values, jnp.transpose(modulation, (1, 0, 2)), w_qkv, w_out, qk_gain)


def solution(mesh):
    placed = (
        P("tm", "patch", None),
        P(None, "patch", "tm"),
        P(None, "patch", "tm"),
        P(),
        P(None, None, "tm", None),
        P(None, "tm", None),
        P(),
    )
    return jax.shard_map(
        functools.partial(local, mesh.shape["tm"], mesh.shape["patch"]),
        mesh=mesh, in_specs=placed, out_specs=P("tm", "patch", None), check_vma=False,
    )
```

```python
import functools

import jax
import jax.numpy as jnp
from jax import lax
from jax.experimental import pallas as pl
from jax.experimental.pallas import tpu as pltpu
from jax.sharding import PartitionSpec as P

HEAD_DIM = 72
EPS = 1e-06
MESH = pl.DeviceIdType.MESH
F32 = jnp.float32
BF16 = jnp.bfloat16
NT = (((1,), (1,)), ((), ()))
NN = (((1,), (0,)), ((), ()))


def head_of(index, heads):
    total = jnp.zeros_like(index)
    for head in range(1, heads + 1):
        total = total + jnp.where(index >= head * HEAD_DIM, 1, 0)
    return total


def split_dot(left, right):
    high = left.astype(BF16)
    low = (left - high.astype(F32)).astype(BF16)
    return lax.dot_general(high, right, NN, preferred_element_type=F32) + lax.dot_general(
        low, right, NN, preferred_element_type=F32
    )


def kernel(
    n_tm, n_patch, width, wide, parts,
    stream_ref, old_k_ref, old_v_ref, mod_ref, w_qkv_ref, w_out_ref, gain_ref,
    out_ref,
    wq, wo, old, mod, gains, own, buf, stage, acc, xg0, *rest_refs,
):
    n_part = len(parts)
    rest_refs = list(rest_refs)

    def take():
        return [rest_refs.pop(0) for _ in range(n_part)]

    xg1, chip_sum, all_sum, qbd = take(), take(), take(), take()
    partial = [take(), take()]
    rp, sx, rx = [take(), take()], [take(), take()], [take(), take()]
    (w_sem, in_sem, kv_send, kv_recv, ag_send_x, ag_send_p, ag_recv,
     rs_send_p, rs_recv_p, rs_send_x, rs_recv_x) = rest_refs
    frames, rows = old_k_ref.shape[0], old_k_ref.shape[1]
    depth = stream_ref.shape[2]
    heads = width // HEAD_DIM
    held = w_out_ref.shape[1]
    packed = frames * width
    main = rows // 16 * 16
    tail = rows - main
    n_chip = n_tm // 2
    n_line = n_patch // 2
    upper = rows // 16 * 16
    cuts = ((0, upper), (upper, 2 * rows - upper))
    scale = HEAD_DIM ** (-0.5)

    t = lax.axis_index("tm")
    chip, core = lax.div(t, 2), lax.rem(t, 2)
    partner = chip * 2 + 1 - core
    p = lax.axis_index("patch")
    a, b = lax.div(p, 2), lax.rem(p, 2)
    beside = a * 2 + 1 - b

    def other_chip(j):
        return lax.rem(chip + j, n_chip)

    inputs = [
        pltpu.make_async_copy(old_k_ref, old.at[0], in_sem.at[0]),
        pltpu.make_async_copy(old_v_ref, old.at[1], in_sem.at[1]),
        pltpu.make_async_copy(stream_ref.at[0], xg0.at[t], in_sem.at[2]),
        pltpu.make_async_copy(mod_ref, mod, in_sem.at[3]),
        pltpu.make_async_copy(gain_ref, gains, in_sem.at[4]),
    ]
    loads = []
    for block in range(2):
        for c in range(3):
            loads.append(pltpu.make_async_copy(
                w_qkv_ref.at[block, c], wq.at[block, c, pl.ds(0, held)], w_sem.at[block * 4 + c]))
        loads.append(pltpu.make_async_copy(
            w_out_ref.at[block], wo.at[block, pl.ds(0, held)], w_sem.at[block * 4 + 3]))
    for load in inputs + loads:
        load.start()

    barrier = pltpu.get_barrier_semaphore()

    def greet(**where):
        pl.semaphore_signal(barrier, inc=1, device_id=where, device_id_type=MESH)

    greet(tm=partner)
    greet(patch=beside)
    for j in range(1, n_chip):
        greet(tm=other_chip(j) * 2 + core)

    @pl.when(a > 0)
    def _():
        greet(patch=p - 2)

    @pl.when(a < n_line - 1)
    def _():
        greet(patch=p + 2)

    def window(frame):
        low = min(frame * width // 128 * 128, packed - wide)
        return low, frame * width - low

    def pack(slot):
        keys, values = acc[0], acc[1]
        slot[...] = jnp.concatenate(
            [keys[:main], values[:main], keys[main:], values[main:]], axis=0).astype(BF16)

    def place(which, frame, value):
        low, offset = window(frame)
        if offset:
            value = pltpu.roll(value, offset, 1)
        acc[which, :, low:low + wide] += value

    def stale(which):
        inputs[which].wait()
        for frame in range(frames):
            stage[which, :, 0:width] = old[which, frame].astype(F32)
            place(which, frame, stage[which])

    acc[...] = jnp.zeros_like(acc)
    stage[...] = jnp.zeros_like(stage)
    stale(0)
    own[0:main] = acc[0, 0:main].astype(BF16)

    met = 1 + n_chip + jnp.where(a > 0, 1, 0) + jnp.where(a < n_line - 1, 1, 0)
    pl.semaphore_wait(barrier, met)

    def remote(src, dst, send, recv, where):
        return pltpu.make_async_remote_copy(
            src_ref=src, dst_ref=dst, send_sem=send, recv_sem=recv, device_id=where, device_id_type=MESH)

    pending = []

    def started(copy):
        copy.start()
        pending.append(copy)

    def kv_copy(src, line, side, cut, kind, step, **where):
        first, count = cuts[cut]
        rows_of = pl.ds(first, count)
        return remote(src.at[rows_of], buf.at[side, line, rows_of], kv_send.at[kind, step, cut],
                      kv_recv.at[side, line, cut], where)

    def kv_arrived(line, side, cut):
        kv_copy(own, line, side, cut, 0, 0, patch=beside).wait_recv()

    def move(copy, go):
        copy.start() if go else copy.wait_send()

    def spot_on_line(line):
        return jnp.clip(line, 0, n_line - 1)

    even = n_line == 4
    at_end = (a == 0) | (a == n_line - 1)
    inward = jnp.where(a == 0, 1, a - 1)
    outward = jnp.where(a == 1, 0, n_line - 1)
    far_end = jnp.where(a == 1, n_line - 1, 0)

    def relay(step, cut, go):
        for kind, sign in ((0, 1), (1, -1)):
            origin = a - sign * step
            onward = a + sign
            line = spot_on_line(origin)
            src = buf.at[b, line] if step else own
            here = (origin >= 0) & (origin < n_line)

            if step:
                @pl.when(here)
                def _():
                    if go:
                        kv_arrived(line, b, cut)

                across = here
                if even and step == 1:
                    across = here & (origin != 0) & (origin != n_line - 1)
                if even and step == 2:
                    across = here & at_end
                if even and step == n_line - 1 and cut == 1:
                    across = None
                if across is not None:
                    @pl.when(across)
                    def _():
                        move(kv_copy(src, line, b, cut, 2 + kind, step, patch=beside), go)

            @pl.when(here & (onward >= 0) & (onward < n_line))
            def _():
                move(kv_copy(src, line, b, cut, kind, step, patch=spot_on_line(onward) * 2 + b), go)
        if step == 0:
            move(kv_copy(own, a, b, cut, 2, 0, patch=beside), go)

    def relay_across(go):
        if even:
            @pl.when(jnp.logical_not(at_end))
            def _():
                for cut in (1, 0):
                    move(kv_copy(buf.at[b, far_end], far_end, b, cut, 2, 2, patch=beside), go)

    def relay_end(cut, go):
        if even:
            @pl.when(at_end)
            def _():
                if go:
                    kv_arrived(a, 1 - b, cut)
                move(kv_copy(buf.at[1 - b, a], a, 1 - b, cut, 4, 0, patch=inward * 2 + b), go)

    def relay_far(go):
        if even:
            @pl.when(jnp.logical_not(at_end))
            def _():
                if go:
                    kv_arrived(far_end, 1 - b, 1)
                move(kv_copy(buf.at[1 - b, far_end], far_end, 1 - b, 1, 4, 1, patch=outward * 2 + b), go)

    def final_waits():
        for line in range(n_line):
            for cut in range(2):
                forwarded = False
                if even and line in (0, n_line - 1):
                    forwarded = at_end & (a == line)
                    if cut == 1:
                        forwarded = forwarded | (jnp.logical_not(at_end) & (far_end == line))

                if forwarded is False:
                    kv_arrived(line, 1 - b, cut)
                else:
                    @pl.when(jnp.logical_not(forwarded))
                    def _():
                        kv_arrived(line, 1 - b, cut)

    def gather_start(phase, src, xg):
        for j in range(1, n_chip):
            started(remote(src, xg.at[t], ag_send_x.at[phase, j], ag_recv.at[phase, t],
                           {"tm": other_chip(j) * 2 + core}))
        started(remote(src, xg.at[t], ag_send_p.at[phase, 0], ag_recv.at[phase, t], {"tm": partner}))

    def gather_arrived(phase, xg, frame):
        remote(xg.at[frame], xg.at[frame], ag_send_p.at[phase, 0], ag_recv.at[phase, frame],
               {"tm": partner}).wait_recv()

    def gather_forward(phase, xg):
        for j in range(1, n_chip):
            frame = other_chip(j) * 2 + core
            gather_arrived(phase, xg, frame)
            started(remote(xg.at[frame], xg.at[frame], ag_send_p.at[phase, j], ag_recv.at[phase, frame],
                           {"tm": partner}))

    def gather_finish(phase, xg):
        for j in range(n_chip):
            gather_arrived(phase, xg, other_chip(j) * 2 + 1 - core)

    relay(0, 0, True)
    inputs[2].wait()
    gather_start(0, xg0.at[t], xg0)
    stale(1)
    own[main:] = jnp.concatenate([acc[1, 0:main], acc[0, main:], acc[1, main:]], axis=0).astype(BF16)
    relay(0, 1, True)

    features = lax.broadcasted_iota(jnp.int32, (wide, wide), 0)
    columns = lax.broadcasted_iota(jnp.int32, (wide, wide), 1)
    same_head = (head_of(features, heads) == head_of(columns, heads)) & (features < width) & (columns < width)
    group = jnp.where(same_head, 1.0, 0.0).astype(BF16)
    lane = lax.broadcasted_iota(jnp.int32, (1, wide), 1)
    lane_head = head_of(lane, heads)
    down = lax.broadcasted_iota(jnp.int32, (HEAD_DIM, wide), 0)
    over = lax.broadcasted_iota(jnp.int32, (HEAD_DIM, wide), 1)
    over_head = head_of(over, heads)
    spread = jnp.where((over - HEAD_DIM * over_head == down) & (over_head < heads), 1.0, 0.0).astype(BF16)

    def gain_row(block, which):
        gain = gains[block, which:which + 1, :]
        first = gain.astype(BF16)
        rest = gain - first.astype(F32)
        return lax.dot_general(first, spread, NN, preferred_element_type=F32) + split_dot(rest, spread)

    if wide > held:
        wq[:, :, held:, :] = jnp.zeros((2, 3, wide - held, depth), BF16)
        wo[:, held:, :] = jnp.zeros((2, wide - held, depth), BF16)
    inputs[3].wait()
    inputs[4].wait()
    gain_rows = [[gain_row(block, c) for c in range(2)] for block in range(2)]

    def modulated(block, xg):
        shift, gain = mod[0, block:block + 1], 1.0 + mod[1, block:block + 1]
        out = []
        for frame in range(frames):
            values = xg[frame].astype(F32)
            center = jnp.mean(values, axis=-1, keepdims=True)
            values = values - center
            spread_ = jnp.mean(values * values, axis=-1, keepdims=True)
            out.append(values * lax.rsqrt(spread_ + EPS) * gain + shift)
        return jnp.concatenate(out, axis=0).astype(BF16)

    def projections(block, hmod):
        raw = lax.dot_general(
            hmod, wq[block].reshape(3 * wide, depth), NT, preferred_element_type=F32)
        out = []
        for c in range(2):
            piece = raw[:, c * wide:(c + 1) * wide]
            square = split_dot(piece * piece, group) * (1.0 / HEAD_DIM)
            out.append(piece * lax.rsqrt(square + EPS) * gain_rows[block][c])
        return out + [raw[:, 2 * wide:]]

    def heads_out(block, half, attn):
        count = parts[half][1]
        product = lax.dot_general(
            jnp.concatenate(attn, axis=0).astype(BF16), wo[block], NN, preferred_element_type=F32)
        for frame in range(frames):
            partial[block][half][frame] = product[frame * count:(frame + 1) * count].astype(BF16)

    def sum_start(block, half):
        phase = block * n_part + half
        part, inbox = partial[block][half], rp[block][half]
        for j in list(range(1, n_chip)) + [0]:
            to = other_chip(j)
            started(remote(part.at[to * 2 + 1 - core], inbox.at[to], rs_send_p.at[phase, j], rs_recv_p.at[phase, to],
                           {"tm": partner}))

    def sum_arrived(phase, inbox, to):
        remote(inbox.at[to], inbox.at[to], rs_send_p.at[phase, 0], rs_recv_p.at[phase, to],
               {"tm": partner}).wait_recv()

    def sum_across(block, half):
        phase = block * n_part + half
        part, inbox, outbox = partial[block][half], rp[block][half], sx[block][half]
        for j in range(1, n_chip):
            to = other_chip(j)
            sum_arrived(phase, inbox, to)
            outbox[j - 1] = (part[to * 2 + core].astype(F32) + inbox[to].astype(F32)).astype(BF16)
            started(remote(outbox.at[j - 1], rx[block][half].at[j - 1], rs_send_x.at[phase, j - 1],
                           rs_recv_x.at[phase, j - 1], {"tm": to * 2 + core}))

    def all_across(half):
        part, inbox, outbox = partial[0][half], rp[0][half], chip_sum[half]
        for j in range(n_chip):
            to = other_chip(j)
            sum_arrived(half, inbox, to)
            outbox[to] = (part[to * 2 + core].astype(F32) + inbox[to].astype(F32)).astype(BF16)
        for j in range(1, n_chip):
            started(remote(outbox, all_sum[half].at[j - 1], rs_send_x.at[half, j - 1],
                           rs_recv_x.at[half, j - 1], {"tm": other_chip(j) * 2 + core}))

    def middle(half):
        first_row, count = parts[half]
        for j in range(1, n_chip):
            remote(chip_sum[half], all_sum[half].at[j - 1], rs_send_x.at[half, j - 1],
                   rs_recv_x.at[half, j - 1], {"tm": partner}).wait_recv()
        for c in range(n_chip):
            frame = c * 2 + core
            total = chip_sum[half][c].astype(F32)
            for j in range(1, n_chip):
                total = total + all_sum[half][j - 1, c].astype(F32)
            mine = xg0[frame].astype(F32)[first_row:first_row + count]
            xg1[half][frame] = (mine + mod[2, 0:1] * total).astype(BF16)
            started(remote(xg1[half].at[frame], xg1[half].at[frame], ag_send_p.at[1 + half, c],
                           ag_recv.at[1 + half, frame], {"tm": partner}))

    def sum_finish(block, half):
        phase = block * n_part + half
        sum_arrived(phase, rp[block][half], chip)
        total = partial[block][half][t].astype(F32) + rp[block][half][chip].astype(F32)
        for j in range(1, n_chip):
            remote(sx[block][half].at[j - 1], rx[block][half].at[j - 1], rs_send_x.at[phase, j - 1],
                   rs_recv_x.at[phase, j - 1], {"tm": partner}).wait_recv()
            total = total + rx[block][half][j - 1].astype(F32)
        return total

    gather_forward(0, xg0)
    if n_line > 1:
        relay(1, 0, True)
        relay_end(0, True)
    gather_finish(0, xg0)
    hmod = modulated(0, xg0)
    if n_line > 1:
        relay(1, 1, True)
        relay_end(1, True)
    for load in loads[:3]:
        load.wait()
    query, keys, values = projections(0, hmod)
    if n_line > 2:
        relay(2, 0, True)
    acc[...] = jnp.zeros_like(acc)
    for frame in range(frames):
        place(0, frame, keys[frame * rows:(frame + 1) * rows])
        place(1, frame, values[frame * rows:(frame + 1) * rows])
        _, offset = window(frame)
        for half, (first_row, count) in enumerate(parts):
            start = frame * rows + first_row
            some = query[start:start + count]
            some = jnp.concatenate([jnp.where(lane_head == head, some, 0.0) for head in range(heads)], axis=0)
            if offset:
                some = pltpu.roll(some, offset, 1)
            qbd[half][frame] = some.astype(BF16)
    pack(buf.at[b, a])
    for step in range(2, n_line):
        for cut in range(2):
            if (step, cut) != (2, 0):
                relay(step, cut, True)
        if step == 2:
            relay_across(True)
    relay_far(True)
    for load in loads[3:]:
        load.wait()
    final_waits()

    spot = lax.broadcasted_iota(jnp.int32, (1, n_patch * 2 * tail), 1)
    real = (lax.rem(spot, 2 * tail) < tail)

    def spatial(frame, half):
        count = parts[half][1]
        low, offset = window(frame)
        keys = buf[:, :, 0:main, low:low + wide].reshape(n_patch * main, wide)
        values = buf[:, :, main:2 * main, low:low + wide].reshape(n_patch * main, wide)
        rest = buf[:, :, 2 * main:, low:low + wide].reshape(n_patch * 2 * tail, wide)
        query = qbd[half][frame]
        first = lax.dot_general(query, keys, NT, preferred_element_type=F32)
        second = lax.dot_general(query, rest, NT, preferred_element_type=F32)
        second = jnp.where(real, second, -1e30)
        top = jnp.maximum(jnp.max(first, axis=-1, keepdims=True), jnp.max(second, axis=-1, keepdims=True))
        first = jnp.exp((first - top) * scale)
        second = jnp.exp((second - top) * scale)
        norm = jnp.sum(first, axis=-1, keepdims=True) + jnp.sum(second, axis=-1, keepdims=True)
        second = pltpu.roll(second, tail, 1)
        mixed = lax.dot_general(first.astype(BF16), values, NN, preferred_element_type=F32)
        mixed = mixed + lax.dot_general(second.astype(BF16), rest, NN, preferred_element_type=F32)
        mixed = mixed / norm
        total = jnp.zeros((count, wide), F32)
        for head in range(heads):
            start = offset + head * HEAD_DIM
            inside = (lane >= start) & (lane < start + HEAD_DIM)
            total = total + jnp.where(inside, mixed[head * count:(head + 1) * count], 0.0)
        return pltpu.roll(total, wide - offset, 1) if offset else total

    def temporal(half, query, keys, values):
        count = parts[half][1]
        query, keys, values = [x.astype(BF16).astype(F32) for x in (query, keys, values)]
        out = []
        for frame in range(frames):
            one = query[frame * count:(frame + 1) * count]
            products = jnp.concatenate(
                [one * keys[g * count:(g + 1) * count] for g in range(frames)], axis=0)
            products = split_dot(products, group) * scale
            scores = [products[g * count:(g + 1) * count] for g in range(frames)]
            top = functools.reduce(jnp.maximum, scores)
            scores = [jnp.exp(score - top) for score in scores]
            norm = 1.0 / functools.reduce(jnp.add, scores)
            total = jnp.zeros((count, wide), F32)
            for g in range(frames):
                weight = (scores[g] * norm).astype(BF16).astype(F32)
                total = total + weight * values[g * count:(g + 1) * count]
            out.append(total)
        return out

    def finish(half):
        return xg1[half][t].astype(F32) + mod[2, 1:2] * sum_finish(1, half)

    for half in range(n_part):
        attn = []
        for frame in range(frames):
            attn.append(spatial(frame, half))
            if half and frame == frames // 2 - 1:
                all_across(half - 1)
        heads_out(0, half, attn)
        sum_start(0, half)
    middle(0)
    all_across(n_part - 1)
    for half in range(n_part):
        gather_finish(1 + half, xg1[half])
        hmod = modulated(1, xg1[half])
        if half + 1 < n_part:
            middle(half + 1)
        triple = projections(1, hmod)
        if half:
            sum_across(1, half - 1)
        heads_out(1, half, temporal(half, *triple))
        sum_start(1, half)
    sum_across(1, n_part - 1)
    result = [finish(half) for half in range(n_part)]
    out_ref[0] = jnp.concatenate(result, axis=0).astype(BF16)

    for copy in pending:
        copy.wait_send()
    for step in range(n_line):
        for cut in range(2):
            relay(step, cut, False)
    for cut in range(2):
        relay_end(cut, False)
    relay_across(False)
    relay_far(False)


def local(n_tm, n_patch, stream, stale_keys, stale_values, modulation, w_qkv, w_out, qk_gain):
    frames, rows, width = stale_keys.shape
    depth = stream.shape[2]
    extra = -width % 16
    if extra:
        w_qkv = jnp.pad(w_qkv, ((0, 0), (0, 0), (0, extra), (0, 0)))
        w_out = jnp.pad(w_out, ((0, 0), (0, extra), (0, 0)))
    wide = max((frame * width % 128 + width + 127) // 128 * 128 for frame in range(frames))
    heads = width // HEAD_DIM
    n_chip, n_line = n_tm // 2, n_patch // 2
    cut = (rows // 2 + 15) // 16 * 16
    parts = ((0, cut), (cut, rows - cut))
    n_part = len(parts)
    vmem = pl.BlockSpec(memory_space=pltpu.VMEM)
    hbm = pl.BlockSpec(memory_space=pltpu.HBM)
    far = max(n_chip - 1, 1)

    def each(*lead):
        return [pltpu.VMEM((*lead, count, depth), BF16) for _, count in parts]

    dma = pltpu.SemaphoreType.DMA
    return pl.pallas_call(
        functools.partial(kernel, n_tm, n_patch, width, wide, parts),
        out_shape=jax.ShapeDtypeStruct(stream.shape, BF16),
        in_specs=[hbm] * 7,
        out_specs=vmem,
        scratch_shapes=[
            pltpu.VMEM((2, 3, wide, depth), BF16),
            pltpu.VMEM((2, wide, depth), BF16),
            pltpu.VMEM((2, frames, rows, width), BF16),
            pltpu.VMEM((3, 2, depth), F32),
            pltpu.VMEM((2, 2, HEAD_DIM), F32),
            pltpu.VMEM((2 * rows, frames * width), BF16),
            pltpu.VMEM((2, n_line, 2 * rows, frames * width), BF16),
            pltpu.VMEM((2, rows, wide), F32),
            pltpu.VMEM((2, rows, frames * width), F32),
            pltpu.VMEM((frames, rows, depth), BF16),
            *each(frames),
            *each(n_chip),
            *each(far, n_chip),
            *[pltpu.VMEM((frames, heads * count, wide), BF16) for _, count in parts],
            *each(frames), *each(frames),
            *each(n_chip), *each(n_chip),
            *each(far), *each(far),
            *each(far), *each(far),
            dma((8,)),
            dma((5,)),
            dma((5, max(n_line, 2), 2)),
            dma((2, n_line, 2)),
            dma((1 + n_part, n_chip)),
            dma((1 + n_part, n_chip)),
            dma((1 + n_part, n_tm)),
            dma((2 * n_part, n_chip)),
            dma((2 * n_part, n_chip)),
            dma((2 * n_part, far)),
            dma((2 * n_part, far)),
        ],
        compiler_params=pltpu.CompilerParams(
            collective_id=0, has_side_effects=True, vmem_limit_bytes=56 * 1024 * 1024),
        cost_estimate=pl.CostEstimate(flops=4_000_000_000, bytes_accessed=8_000_000, transcendentals=1_000_000),
    )(stream, stale_keys, stale_values, jnp.transpose(modulation, (1, 0, 2)), w_qkv, w_out, qk_gain)


def solution(mesh):
    placed = (
        P("tm", "patch", None),
        P(None, "patch", "tm"),
        P(None, "patch", "tm"),
        P(),
        P(None, None, "tm", None),
        P(None, "tm", None),
        P(),
    )
    return jax.shard_map(
        functools.partial(local, mesh.shape["tm"], mesh.shape["patch"]),
        mesh=mesh, in_specs=placed, out_specs=P("tm", "patch", None), check_vma=False,
    )
```

```python
import functools

import jax
import jax.numpy as jnp
from jax import lax
from jax.experimental import pallas as pl
from jax.experimental.pallas import tpu as pltpu
from jax.sharding import PartitionSpec as P

HEAD_DIM = 72
EPS = 1e-06
MESH = pl.DeviceIdType.MESH
F32 = jnp.float32
BF16 = jnp.bfloat16
NT = (((1,), (1,)), ((), ()))
NN = (((1,), (0,)), ((), ()))


def head_of(index, heads):
    total = jnp.zeros_like(index)
    for head in range(1, heads + 1):
        total = total + jnp.where(index >= head * HEAD_DIM, 1, 0)
    return total


def split_dot(left, right):
    high = left.astype(BF16)
    low = (left - high.astype(F32)).astype(BF16)
    return lax.dot_general(high, right, NN, preferred_element_type=F32) + lax.dot_general(
        low, right, NN, preferred_element_type=F32
    )


def kernel(
    n_tm, n_patch, width, wide, parts,
    stream_ref, old_k_ref, old_v_ref, mod_ref, w_qkv_ref, w_out_ref, gain_ref,
    out_ref,
    wq, wo, old, mod, gains, own, buf, stage, acc, xg0, *rest_refs,
):
    n_part = len(parts)
    rest_refs = list(rest_refs)

    def take():
        return [rest_refs.pop(0) for _ in range(n_part)]

    xg1, chip_sum, all_sum, qbd, early = take(), take(), take(), take(), take()
    partial = [take(), take()]
    rp, sx, rx = [take(), take()], [take(), take()], [take(), take()]
    (w_sem, in_sem, kv_send, kv_recv, ag_send_x, ag_send_p, ag_recv,
     rs_send_p, rs_recv_p, rs_send_x, rs_recv_x) = rest_refs
    frames, rows = old_k_ref.shape[0], old_k_ref.shape[1]
    depth = stream_ref.shape[2]
    heads = width // HEAD_DIM
    held = w_out_ref.shape[1]
    packed = frames * width
    main = rows // 16 * 16
    tail = rows - main
    n_chip = n_tm // 2
    n_line = n_patch // 2
    upper = rows // 16 * 16
    cuts = ((0, upper), (upper, 2 * rows - upper))
    scale = HEAD_DIM ** (-0.5)

    t = lax.axis_index("tm")
    chip, core = lax.div(t, 2), lax.rem(t, 2)
    partner = chip * 2 + 1 - core
    p = lax.axis_index("patch")
    a, b = lax.div(p, 2), lax.rem(p, 2)
    beside = a * 2 + 1 - b

    def other_chip(j):
        return lax.rem(chip + j, n_chip)

    inputs = [
        pltpu.make_async_copy(old_k_ref, old.at[0], in_sem.at[0]),
        pltpu.make_async_copy(old_v_ref, old.at[1], in_sem.at[1]),
        pltpu.make_async_copy(stream_ref.at[0], xg0.at[t], in_sem.at[2]),
        pltpu.make_async_copy(mod_ref, mod, in_sem.at[3]),
        pltpu.make_async_copy(gain_ref, gains, in_sem.at[4]),
    ]
    loads = []
    for block in range(2):
        for c in range(3):
            loads.append(pltpu.make_async_copy(
                w_qkv_ref.at[block, c], wq.at[block, c, pl.ds(0, held)], w_sem.at[block * 4 + c]))
        loads.append(pltpu.make_async_copy(
            w_out_ref.at[block], wo.at[block, pl.ds(0, held)], w_sem.at[block * 4 + 3]))
    for load in inputs + loads:
        load.start()

    barrier = pltpu.get_barrier_semaphore()

    def greet(**where):
        pl.semaphore_signal(barrier, inc=1, device_id=where, device_id_type=MESH)

    greet(tm=partner)
    greet(patch=beside)
    for j in range(1, n_chip):
        greet(tm=other_chip(j) * 2 + core)

    @pl.when(a > 0)
    def _():
        greet(patch=p - 2)

    @pl.when(a < n_line - 1)
    def _():
        greet(patch=p + 2)

    def window(frame):
        low = min(frame * width // 128 * 128, packed - wide)
        return low, frame * width - low

    def pack(slot):
        keys, values = acc[0], acc[1]
        slot[...] = jnp.concatenate(
            [keys[:main], values[:main], keys[main:], values[main:]], axis=0).astype(BF16)

    def place(which, frame, value):
        low, offset = window(frame)
        if offset:
            value = pltpu.roll(value, offset, 1)
        acc[which, :, low:low + wide] += value

    def stale(which):
        inputs[which].wait()
        for frame in range(frames):
            stage[which, :, 0:width] = old[which, frame].astype(F32)
            place(which, frame, stage[which])

    acc[...] = jnp.zeros_like(acc)
    stage[...] = jnp.zeros_like(stage)
    stale(0)
    own[0:main] = acc[0, 0:main].astype(BF16)

    met = 1 + n_chip + jnp.where(a > 0, 1, 0) + jnp.where(a < n_line - 1, 1, 0)
    pl.semaphore_wait(barrier, met)

    def remote(src, dst, send, recv, where):
        return pltpu.make_async_remote_copy(
            src_ref=src, dst_ref=dst, send_sem=send, recv_sem=recv, device_id=where, device_id_type=MESH)

    pending = []

    def started(copy):
        copy.start()
        pending.append(copy)

    def kv_copy(src, line, side, cut, kind, step, **where):
        first, count = cuts[cut]
        rows_of = pl.ds(first, count)
        return remote(src.at[rows_of], buf.at[side, line, rows_of], kv_send.at[kind, step, cut],
                      kv_recv.at[side, line, cut], where)

    def kv_arrived(line, side, cut):
        kv_copy(own, line, side, cut, 0, 0, patch=beside).wait_recv()

    def move(copy, go):
        copy.start() if go else copy.wait_send()

    def spot_on_line(line):
        return jnp.clip(line, 0, n_line - 1)

    even = n_line == 4
    at_end = (a == 0) | (a == n_line - 1)
    inward = jnp.where(a == 0, 1, a - 1)
    outward = jnp.where(a == 1, 0, n_line - 1)
    far_end = jnp.where(a == 1, n_line - 1, 0)

    def relay(step, cut, go):
        for kind, sign in ((0, 1), (1, -1)):
            origin = a - sign * step
            onward = a + sign
            line = spot_on_line(origin)
            src = buf.at[b, line] if step else own
            here = (origin >= 0) & (origin < n_line)

            if step:
                @pl.when(here)
                def _():
                    if go:
                        kv_arrived(line, b, cut)

                across = here
                if even and step == 1:
                    across = here & (origin != 0) & (origin != n_line - 1)
                if even and step == 2:
                    across = here & at_end
                if even and step == n_line - 1 and cut == 1:
                    across = None
                if across is not None:
                    @pl.when(across)
                    def _():
                        move(kv_copy(src, line, b, cut, 2 + kind, step, patch=beside), go)

            @pl.when(here & (onward >= 0) & (onward < n_line))
            def _():
                move(kv_copy(src, line, b, cut, kind, step, patch=spot_on_line(onward) * 2 + b), go)
        if step == 0:
            move(kv_copy(own, a, b, cut, 2, 0, patch=beside), go)

    def relay_across(go):
        if even:
            @pl.when(jnp.logical_not(at_end))
            def _():
                for cut in (1, 0):
                    move(kv_copy(buf.at[b, far_end], far_end, b, cut, 2, 2, patch=beside), go)

    def relay_end(cut, go):
        if even:
            @pl.when(at_end)
            def _():
                if go:
                    kv_arrived(a, 1 - b, cut)
                move(kv_copy(buf.at[1 - b, a], a, 1 - b, cut, 4, 0, patch=inward * 2 + b), go)

    def relay_far(go):
        if even:
            @pl.when(jnp.logical_not(at_end))
            def _():
                if go:
                    kv_arrived(far_end, 1 - b, 1)
                move(kv_copy(buf.at[1 - b, far_end], far_end, 1 - b, 1, 4, 1, patch=outward * 2 + b), go)

    def final_waits():
        for line in range(n_line):
            for cut in range(2):
                forwarded = False
                if even and line in (0, n_line - 1):
                    forwarded = at_end & (a == line)
                    if cut == 1:
                        forwarded = forwarded | (jnp.logical_not(at_end) & (far_end == line))

                if forwarded is False:
                    kv_arrived(line, 1 - b, cut)
                else:
                    @pl.when(jnp.logical_not(forwarded))
                    def _():
                        kv_arrived(line, 1 - b, cut)

    def gather_start(phase, src, xg):
        for j in range(1, n_chip):
            started(remote(src, xg.at[t], ag_send_x.at[phase, j], ag_recv.at[phase, t],
                           {"tm": other_chip(j) * 2 + core}))
        started(remote(src, xg.at[t], ag_send_p.at[phase, 0], ag_recv.at[phase, t], {"tm": partner}))

    def gather_arrived(phase, xg, frame):
        remote(xg.at[frame], xg.at[frame], ag_send_p.at[phase, 0], ag_recv.at[phase, frame],
               {"tm": partner}).wait_recv()

    def gather_forward(phase, xg):
        for j in range(1, n_chip):
            frame = other_chip(j) * 2 + core
            gather_arrived(phase, xg, frame)
            started(remote(xg.at[frame], xg.at[frame], ag_send_p.at[phase, j], ag_recv.at[phase, frame],
                           {"tm": partner}))

    def gather_finish(phase, xg):
        for j in range(n_chip):
            gather_arrived(phase, xg, other_chip(j) * 2 + 1 - core)

    relay(0, 0, True)
    inputs[2].wait()
    gather_start(0, xg0.at[t], xg0)
    stale(1)
    own[main:] = jnp.concatenate([acc[1, 0:main], acc[0, main:], acc[1, main:]], axis=0).astype(BF16)
    relay(0, 1, True)

    features = lax.broadcasted_iota(jnp.int32, (wide, wide), 0)
    columns = lax.broadcasted_iota(jnp.int32, (wide, wide), 1)
    same_head = (head_of(features, heads) == head_of(columns, heads)) & (features < width) & (columns < width)
    group = jnp.where(same_head, 1.0, 0.0).astype(BF16)
    lane = lax.broadcasted_iota(jnp.int32, (1, wide), 1)
    lane_head = head_of(lane, heads)
    down = lax.broadcasted_iota(jnp.int32, (HEAD_DIM, wide), 0)
    over = lax.broadcasted_iota(jnp.int32, (HEAD_DIM, wide), 1)
    over_head = head_of(over, heads)
    spread = jnp.where((over - HEAD_DIM * over_head == down) & (over_head < heads), 1.0, 0.0).astype(BF16)

    def gain_row(block, which):
        gain = gains[block, which:which + 1, :]
        first = gain.astype(BF16)
        rest = gain - first.astype(F32)
        return lax.dot_general(first, spread, NN, preferred_element_type=F32) + split_dot(rest, spread)

    if wide > held:
        wq[:, :, held:, :] = jnp.zeros((2, 3, wide - held, depth), BF16)
        wo[:, held:, :] = jnp.zeros((2, wide - held, depth), BF16)
    inputs[3].wait()
    inputs[4].wait()
    gain_rows = [[gain_row(block, c) for c in range(2)] for block in range(2)]

    def modulated(block, xg):
        shift, gain = mod[0, block:block + 1], 1.0 + mod[1, block:block + 1]
        out = []
        for frame in range(frames):
            values = xg[frame].astype(F32)
            center = jnp.mean(values, axis=-1, keepdims=True)
            values = values - center
            spread_ = jnp.mean(values * values, axis=-1, keepdims=True)
            out.append(values * lax.rsqrt(spread_ + EPS) * gain + shift)
        return jnp.concatenate(out, axis=0).astype(BF16)

    def projections(block, hmod):
        raw = lax.dot_general(
            hmod, wq[block].reshape(3 * wide, depth), NT, preferred_element_type=F32)
        out = []
        for c in range(2):
            piece = raw[:, c * wide:(c + 1) * wide]
            square = split_dot(piece * piece, group) * (1.0 / HEAD_DIM)
            out.append(piece * lax.rsqrt(square + EPS) * gain_rows[block][c])
        return out + [raw[:, 2 * wide:]]

    def heads_out(block, half, attn):
        count = parts[half][1]
        product = lax.dot_general(
            jnp.concatenate(attn, axis=0).astype(BF16), wo[block], NN, preferred_element_type=F32)
        for frame in range(frames):
            partial[block][half][frame] = product[frame * count:(frame + 1) * count].astype(BF16)

    def sum_start(block, half):
        phase = block * n_part + half
        part, inbox = partial[block][half], rp[block][half]
        for j in list(range(1, n_chip)) + [0]:
            to = other_chip(j)
            started(remote(part.at[to * 2 + 1 - core], inbox.at[to], rs_send_p.at[phase, j], rs_recv_p.at[phase, to],
                           {"tm": partner}))

    def sum_arrived(phase, inbox, to):
        remote(inbox.at[to], inbox.at[to], rs_send_p.at[phase, 0], rs_recv_p.at[phase, to],
               {"tm": partner}).wait_recv()

    def sum_across(block, half):
        phase = block * n_part + half
        part, inbox, outbox = partial[block][half], rp[block][half], sx[block][half]
        for j in range(1, n_chip):
            to = other_chip(j)
            sum_arrived(phase, inbox, to)
            outbox[j - 1] = (part[to * 2 + core].astype(F32) + inbox[to].astype(F32)).astype(BF16)
            started(remote(outbox.at[j - 1], rx[block][half].at[j - 1], rs_send_x.at[phase, j - 1],
                           rs_recv_x.at[phase, j - 1], {"tm": to * 2 + core}))

    def all_across(half):
        part, inbox, outbox = partial[0][half], rp[0][half], chip_sum[half]
        for j in range(n_chip):
            to = other_chip(j)
            sum_arrived(half, inbox, to)
            outbox[to] = (part[to * 2 + core].astype(F32) + inbox[to].astype(F32)).astype(BF16)
        for j in range(1, n_chip):
            started(remote(outbox, all_sum[half].at[j - 1], rs_send_x.at[half, j - 1],
                           rs_recv_x.at[half, j - 1], {"tm": other_chip(j) * 2 + core}))

    def middle(half):
        first_row, count = parts[half]
        for j in range(1, n_chip):
            remote(chip_sum[half], all_sum[half].at[j - 1], rs_send_x.at[half, j - 1],
                   rs_recv_x.at[half, j - 1], {"tm": partner}).wait_recv()
        for c in range(n_chip):
            frame = c * 2 + core
            total = chip_sum[half][c].astype(F32)
            for j in range(1, n_chip):
                total = total + all_sum[half][j - 1, c].astype(F32)
            mine = xg0[frame].astype(F32)[first_row:first_row + count]
            xg1[half][frame] = (mine + mod[2, 0:1] * total).astype(BF16)
            started(remote(xg1[half].at[frame], xg1[half].at[frame], ag_send_p.at[1 + half, c],
                           ag_recv.at[1 + half, frame], {"tm": partner}))

    def sum_finish(block, half):
        phase = block * n_part + half
        sum_arrived(phase, rp[block][half], chip)
        total = partial[block][half][t].astype(F32) + rp[block][half][chip].astype(F32)
        for j in range(1, n_chip):
            remote(sx[block][half].at[j - 1], rx[block][half].at[j - 1], rs_send_x.at[phase, j - 1],
                   rs_recv_x.at[phase, j - 1], {"tm": partner}).wait_recv()
            total = total + rx[block][half][j - 1].astype(F32)
        return total

    gather_forward(0, xg0)
    if n_line > 1:
        relay(1, 0, True)
        relay_end(0, True)
    gather_finish(0, xg0)
    hmod = modulated(0, xg0)
    if n_line > 1:
        relay(1, 1, True)
        relay_end(1, True)
    for load in loads[:3]:
        load.wait()
    query, keys, values = projections(0, hmod)
    if n_line > 2:
        relay(2, 0, True)
    acc[...] = jnp.zeros_like(acc)
    for frame in range(frames):
        place(0, frame, keys[frame * rows:(frame + 1) * rows])
        place(1, frame, values[frame * rows:(frame + 1) * rows])
        _, offset = window(frame)
        for half, (first_row, count) in enumerate(parts):
            start = frame * rows + first_row
            some = query[start:start + count]
            some = jnp.concatenate([jnp.where(lane_head == head, some, 0.0) for head in range(heads)], axis=0)
            if offset:
                some = pltpu.roll(some, offset, 1)
            qbd[half][frame] = some.astype(BF16)
    pack(buf.at[b, a])
    for step in range(2, n_line):
        for cut in range(2):
            if (step, cut) != (2, 0):
                relay(step, cut, True)
        if step == 2:
            relay_across(True)
    relay_far(True)

    spot = lax.broadcasted_iota(jnp.int32, (1, n_line * rows + n_line * tail), 1)
    in_main = spot < n_line * main
    in_tail = lax.rem(spot, 2 * tail) < tail
    if n_line * main % (2 * tail):
        in_tail = lax.rem(jnp.maximum(spot - n_line * main, 0), 2 * tail) < tail

    def column_attention(frame, half, side):
        count = parts[half][1]
        low, offset = window(frame)
        rest = buf[side, :, 2 * main:, low:low + wide].reshape(n_line * 2 * tail, wide)
        keys = buf[side, :, 0:main, low:low + wide].reshape(n_line * main, wide)
        values = buf[side, :, main:2 * main, low:low + wide].reshape(n_line * main, wide)
        keys = jnp.concatenate([keys, rest], axis=0)
        values = jnp.concatenate([values, rest], axis=0)
        scores = lax.dot_general(qbd[half][frame], keys, NT, preferred_element_type=F32)
        scores = jnp.where(in_main | in_tail, scores, -1e30)
        top = jnp.max(scores, axis=-1, keepdims=True)
        weights = jnp.exp((scores - top) * scale)
        norm = jnp.sum(weights, axis=-1, keepdims=True)
        moved = jnp.where(in_tail, 0.0, pltpu.roll(weights, tail, 1))
        weights = jnp.where(in_main, weights, moved).astype(BF16)
        mixed = lax.dot_general(weights, values, NN, preferred_element_type=F32)
        out = [jnp.zeros((count, wide), F32), jnp.zeros((count, wide), F32), jnp.ones((count, wide), F32)]
        for head in range(heads):
            start = offset + head * HEAD_DIM
            inside = (lane >= start) & (lane < start + HEAD_DIM)
            of_head = slice(head * count, (head + 1) * count)
            out = [jnp.where(inside, x[of_head], y) for x, y in zip((mixed, top, norm), out)]
        return out

    for half in range(n_part):
        for frame in range(frames):
            for i, value in enumerate(column_attention(frame, half, b)):
                early[half][i, frame] = value
    for load in loads[3:]:
        load.wait()
    final_waits()

    def spatial(frame, half):
        weighted, top, norm = column_attention(frame, half, 1 - b)
        before, top_before, norm_before = [early[half][i, frame] for i in range(3)]
        highest = jnp.maximum(top, top_before)
        now, then = jnp.exp((top - highest) * scale), jnp.exp((top_before - highest) * scale)
        total = (weighted * now + before * then) / (norm * now + norm_before * then)
        _, offset = window(frame)
        return pltpu.roll(total, wide - offset, 1) if offset else total

    def temporal(half, query, keys, values):
        count = parts[half][1]
        query, keys, values = [x.astype(BF16).astype(F32) for x in (query, keys, values)]
        out = []
        for frame in range(frames):
            one = query[frame * count:(frame + 1) * count]
            products = jnp.concatenate(
                [one * keys[g * count:(g + 1) * count] for g in range(frames)], axis=0)
            products = split_dot(products, group) * scale
            scores = [products[g * count:(g + 1) * count] for g in range(frames)]
            top = functools.reduce(jnp.maximum, scores)
            scores = [jnp.exp(score - top) for score in scores]
            norm = 1.0 / functools.reduce(jnp.add, scores)
            total = jnp.zeros((count, wide), F32)
            for g in range(frames):
                weight = (scores[g] * norm).astype(BF16).astype(F32)
                total = total + weight * values[g * count:(g + 1) * count]
            out.append(total)
        return out

    def finish(half):
        return xg1[half][t].astype(F32) + mod[2, 1:2] * sum_finish(1, half)

    for half in range(n_part):
        attn = []
        for frame in range(frames):
            attn.append(spatial(frame, half))
            if half and frame == frames // 2 - 1:
                all_across(half - 1)
        heads_out(0, half, attn)
        sum_start(0, half)
    middle(0)
    all_across(n_part - 1)
    for half in range(n_part):
        gather_finish(1 + half, xg1[half])
        hmod = modulated(1, xg1[half])
        if half + 1 < n_part:
            middle(half + 1)
        triple = projections(1, hmod)
        if half:
            sum_across(1, half - 1)
        heads_out(1, half, temporal(half, *triple))
        sum_start(1, half)
    sum_across(1, n_part - 1)
    result = [finish(half) for half in range(n_part)]
    out_ref[0] = jnp.concatenate(result, axis=0).astype(BF16)

    for copy in pending:
        copy.wait_send()
    for step in range(n_line):
        for cut in range(2):
            relay(step, cut, False)
    for cut in range(2):
        relay_end(cut, False)
    relay_across(False)
    relay_far(False)


def local(n_tm, n_patch, stream, stale_keys, stale_values, modulation, w_qkv, w_out, qk_gain):
    frames, rows, width = stale_keys.shape
    depth = stream.shape[2]
    extra = -width % 16
    if extra:
        w_qkv = jnp.pad(w_qkv, ((0, 0), (0, 0), (0, extra), (0, 0)))
        w_out = jnp.pad(w_out, ((0, 0), (0, extra), (0, 0)))
    wide = max((frame * width % 128 + width + 127) // 128 * 128 for frame in range(frames))
    heads = width // HEAD_DIM
    n_chip, n_line = n_tm // 2, n_patch // 2
    cut = (rows // 2 + 15) // 16 * 16
    parts = ((0, cut), (cut, rows - cut))
    n_part = len(parts)
    vmem = pl.BlockSpec(memory_space=pltpu.VMEM)
    hbm = pl.BlockSpec(memory_space=pltpu.HBM)
    far = max(n_chip - 1, 1)

    def each(*lead):
        return [pltpu.VMEM((*lead, count, depth), BF16) for _, count in parts]

    dma = pltpu.SemaphoreType.DMA
    return pl.pallas_call(
        functools.partial(kernel, n_tm, n_patch, width, wide, parts),
        out_shape=jax.ShapeDtypeStruct(stream.shape, BF16),
        in_specs=[hbm] * 7,
        out_specs=vmem,
        scratch_shapes=[
            pltpu.VMEM((2, 3, wide, depth), BF16),
            pltpu.VMEM((2, wide, depth), BF16),
            pltpu.VMEM((2, frames, rows, width), BF16),
            pltpu.VMEM((3, 2, depth), F32),
            pltpu.VMEM((2, 2, HEAD_DIM), F32),
            pltpu.VMEM((2 * rows, frames * width), BF16),
            pltpu.VMEM((2, n_line, 2 * rows, frames * width), BF16),
            pltpu.VMEM((2, rows, wide), F32),
            pltpu.VMEM((2, rows, frames * width), F32),
            pltpu.VMEM((frames, rows, depth), BF16),
            *each(frames),
            *each(n_chip),
            *each(far, n_chip),
            *[pltpu.VMEM((frames, heads * count, wide), BF16) for _, count in parts],
            *[pltpu.VMEM((3, frames, count, wide), F32) for _, count in parts],
            *each(frames), *each(frames),
            *each(n_chip), *each(n_chip),
            *each(far), *each(far),
            *each(far), *each(far),
            dma((8,)),
            dma((5,)),
            dma((5, max(n_line, 2), 2)),
            dma((2, n_line, 2)),
            dma((1 + n_part, n_chip)),
            dma((1 + n_part, n_chip)),
            dma((1 + n_part, n_tm)),
            dma((2 * n_part, n_chip)),
            dma((2 * n_part, n_chip)),
            dma((2 * n_part, far)),
            dma((2 * n_part, far)),
        ],
        compiler_params=pltpu.CompilerParams(
            collective_id=0, has_side_effects=True, vmem_limit_bytes=56 * 1024 * 1024),
        cost_estimate=pl.CostEstimate(flops=4_000_000_000, bytes_accessed=8_000_000, transcendentals=1_000_000),
    )(stream, stale_keys, stale_values, jnp.transpose(modulation, (1, 0, 2)), w_qkv, w_out, qk_gain)


def solution(mesh):
    placed = (
        P("tm", "patch", None),
        P(None, "patch", "tm"),
        P(None, "patch", "tm"),
        P(),
        P(None, None, "tm", None),
        P(None, "tm", None),
        P(),
    )
    return jax.shard_map(
        functools.partial(local, mesh.shape["tm"], mesh.shape["patch"]),
        mesh=mesh, in_specs=placed, out_specs=P("tm", "patch", None), check_vma=False,
    )
```

```python
import functools

import jax
import jax.numpy as jnp
from jax import lax
from jax.experimental import pallas as pl
from jax.experimental.pallas import tpu as pltpu
from jax.sharding import PartitionSpec as P

HEAD_DIM = 72
EPS = 1e-06
MESH = pl.DeviceIdType.MESH
F32 = jnp.float32
BF16 = jnp.bfloat16
NT = (((1,), (1,)), ((), ()))
NN = (((1,), (0,)), ((), ()))


def head_of(index, heads):
    total = jnp.zeros_like(index)
    for head in range(1, heads + 1):
        total = total + jnp.where(index >= head * HEAD_DIM, 1, 0)
    return total


def split_dot(left, right):
    high = left.astype(BF16)
    low = (left - high.astype(F32)).astype(BF16)
    count = left.shape[0]
    if count % 16 == 0:
        both = lax.dot_general(jnp.concatenate([high, low], axis=0), right, NN, preferred_element_type=F32)
        return both[:count] + both[count:]
    return lax.dot_general(high, right, NN, preferred_element_type=F32) + lax.dot_general(
        low, right, NN, preferred_element_type=F32
    )


def kernel(
    n_tm, n_patch, width, wide, parts,
    stream_ref, old_k_ref, old_v_ref, mod_ref, w_qkv_ref, w_out_ref, gain_ref,
    out_ref,
    wq, wo, old, mod, gains, own, buf, stage, acc, xg0, *rest_refs,
):
    n_part = len(parts)
    rest_refs = list(rest_refs)

    def take():
        return [rest_refs.pop(0) for _ in range(n_part)]

    xg1, chip_sum, all_sum, qbd, early = take(), take(), take(), take(), take()
    partial = [take(), take()]
    rp, sx, rx = [take(), take()], [take(), take()], [take(), take()]
    (w_sem, in_sem, kv_send, kv_recv, ag_send_x, ag_send_p, ag_recv,
     rs_send_p, rs_recv_p, rs_send_x, rs_recv_x) = rest_refs
    frames, rows = old_k_ref.shape[0], old_k_ref.shape[1]
    depth = stream_ref.shape[2]
    heads = width // HEAD_DIM
    held = w_out_ref.shape[1]
    packed = frames * width
    main = rows // 16 * 16
    tail = rows - main
    n_chip = n_tm // 2
    n_line = n_patch // 2
    upper = rows // 16 * 16
    cuts = ((0, upper), (upper, 2 * rows - upper))
    scale = HEAD_DIM ** (-0.5)

    t = lax.axis_index("tm")
    chip, core = lax.div(t, 2), lax.rem(t, 2)
    partner = chip * 2 + 1 - core
    p = lax.axis_index("patch")
    a, b = lax.div(p, 2), lax.rem(p, 2)
    beside = a * 2 + 1 - b

    def other_chip(j):
        return lax.rem(chip + j, n_chip)

    inputs = [
        pltpu.make_async_copy(old_k_ref, old.at[0], in_sem.at[0]),
        pltpu.make_async_copy(old_v_ref, old.at[1], in_sem.at[1]),
        pltpu.make_async_copy(stream_ref.at[0], xg0.at[t], in_sem.at[2]),
        pltpu.make_async_copy(mod_ref, mod, in_sem.at[3]),
        pltpu.make_async_copy(gain_ref, gains, in_sem.at[4]),
    ]
    loads = []
    for block in range(2):
        for c in range(3):
            loads.append(pltpu.make_async_copy(
                w_qkv_ref.at[block, c], wq.at[block, c, pl.ds(0, held)], w_sem.at[block * 4 + c]))
        loads.append(pltpu.make_async_copy(
            w_out_ref.at[block], wo.at[block, pl.ds(0, held)], w_sem.at[block * 4 + 3]))
    for load in inputs + loads:
        load.start()

    barrier = pltpu.get_barrier_semaphore()

    def greet(**where):
        pl.semaphore_signal(barrier, inc=1, device_id=where, device_id_type=MESH)

    greet(tm=partner)
    greet(patch=beside)
    for j in range(1, n_chip):
        greet(tm=other_chip(j) * 2 + core)

    @pl.when(a > 0)
    def _():
        greet(patch=p - 2)

    @pl.when(a < n_line - 1)
    def _():
        greet(patch=p + 2)

    def window(frame):
        low = min(frame * width // 128 * 128, packed - wide)
        return low, frame * width - low

    def pack(slot):
        keys, values = acc[0], acc[1]
        slot[...] = jnp.concatenate(
            [keys[:main], values[:main], keys[main:], values[main:]], axis=0).astype(BF16)

    def place(which, frame, value):
        low, offset = window(frame)
        if offset:
            value = pltpu.roll(value, offset, 1)
        acc[which, :, low:low + wide] += value

    def stale(which):
        inputs[which].wait()
        for frame in range(frames):
            stage[which, :, 0:width] = old[which, frame].astype(F32)
            place(which, frame, stage[which])

    acc[...] = jnp.zeros_like(acc)
    stage[...] = jnp.zeros_like(stage)
    stale(0)
    own[0:main] = acc[0, 0:main].astype(BF16)

    met = 1 + n_chip + jnp.where(a > 0, 1, 0) + jnp.where(a < n_line - 1, 1, 0)
    pl.semaphore_wait(barrier, met)

    def remote(src, dst, send, recv, where):
        return pltpu.make_async_remote_copy(
            src_ref=src, dst_ref=dst, send_sem=send, recv_sem=recv, device_id=where, device_id_type=MESH)

    pending = []

    def started(copy):
        copy.start()
        pending.append(copy)

    def kv_copy(src, line, side, cut, kind, step, **where):
        first, count = cuts[cut]
        rows_of = pl.ds(first, count)
        return remote(src.at[rows_of], buf.at[side, line, rows_of], kv_send.at[kind, step, cut],
                      kv_recv.at[side, line, cut], where)

    def kv_arrived(line, side, cut):
        kv_copy(own, line, side, cut, 0, 0, patch=beside).wait_recv()

    def move(copy, go):
        copy.start() if go else copy.wait_send()

    def spot_on_line(line):
        return jnp.clip(line, 0, n_line - 1)

    even = n_line == 4
    at_end = (a == 0) | (a == n_line - 1)
    inward = jnp.where(a == 0, 1, a - 1)
    outward = jnp.where(a == 1, 0, n_line - 1)
    far_end = jnp.where(a == 1, n_line - 1, 0)

    def relay(step, cut, go):
        for kind, sign in ((0, 1), (1, -1)):
            origin = a - sign * step
            onward = a + sign
            line = spot_on_line(origin)
            src = buf.at[b, line] if step else own
            here = (origin >= 0) & (origin < n_line)

            if step:
                @pl.when(here)
                def _():
                    if go:
                        kv_arrived(line, b, cut)

                across = here
                if even and step == 1:
                    across = here & (origin != 0) & (origin != n_line - 1)
                if even and step == 2:
                    across = here & at_end
                if even and step == n_line - 1 and cut == 1:
                    across = None
                if across is not None:
                    @pl.when(across)
                    def _():
                        move(kv_copy(src, line, b, cut, 2 + kind, step, patch=beside), go)

            @pl.when(here & (onward >= 0) & (onward < n_line))
            def _():
                move(kv_copy(src, line, b, cut, kind, step, patch=spot_on_line(onward) * 2 + b), go)
        if step == 0:
            move(kv_copy(own, a, b, cut, 2, 0, patch=beside), go)

    def relay_across(go):
        if even:
            @pl.when(jnp.logical_not(at_end))
            def _():
                for cut in (1, 0):
                    move(kv_copy(buf.at[b, far_end], far_end, b, cut, 2, 2, patch=beside), go)

    def relay_end(cut, go):
        if even:
            @pl.when(at_end)
            def _():
                if go:
                    kv_arrived(a, 1 - b, cut)
                move(kv_copy(buf.at[1 - b, a], a, 1 - b, cut, 4, 0, patch=inward * 2 + b), go)

    def relay_far(go):
        if even:
            @pl.when(jnp.logical_not(at_end))
            def _():
                if go:
                    kv_arrived(far_end, 1 - b, 1)
                move(kv_copy(buf.at[1 - b, far_end], far_end, 1 - b, 1, 4, 1, patch=outward * 2 + b), go)

    def final_waits():
        for line in range(n_line):
            for cut in range(2):
                forwarded = False
                if even and line in (0, n_line - 1):
                    forwarded = at_end & (a == line)
                    if cut == 1:
                        forwarded = forwarded | (jnp.logical_not(at_end) & (far_end == line))

                if forwarded is False:
                    kv_arrived(line, 1 - b, cut)
                else:
                    @pl.when(jnp.logical_not(forwarded))
                    def _():
                        kv_arrived(line, 1 - b, cut)

    def gather_start(phase, src, xg):
        for j in range(1, n_chip):
            started(remote(src, xg.at[t], ag_send_x.at[phase, j], ag_recv.at[phase, t],
                           {"tm": other_chip(j) * 2 + core}))
        started(remote(src, xg.at[t], ag_send_p.at[phase, 0], ag_recv.at[phase, t], {"tm": partner}))

    def gather_arrived(phase, xg, frame):
        remote(xg.at[frame], xg.at[frame], ag_send_p.at[phase, 0], ag_recv.at[phase, frame],
               {"tm": partner}).wait_recv()

    def gather_forward(phase, xg):
        for j in range(1, n_chip):
            frame = other_chip(j) * 2 + core
            gather_arrived(phase, xg, frame)
            started(remote(xg.at[frame], xg.at[frame], ag_send_p.at[phase, j], ag_recv.at[phase, frame],
                           {"tm": partner}))

    def gather_finish(phase, xg):
        for j in range(n_chip):
            gather_arrived(phase, xg, other_chip(j) * 2 + 1 - core)

    relay(0, 0, True)
    inputs[2].wait()
    gather_start(0, xg0.at[t], xg0)
    stale(1)
    own[main:] = jnp.concatenate([acc[1, 0:main], acc[0, main:], acc[1, main:]], axis=0).astype(BF16)
    relay(0, 1, True)

    features = lax.broadcasted_iota(jnp.int32, (wide, wide), 0)
    columns = lax.broadcasted_iota(jnp.int32, (wide, wide), 1)
    same_head = (head_of(features, heads) == head_of(columns, heads)) & (features < width) & (columns < width)
    group = jnp.where(same_head, 1.0, 0.0).astype(BF16)
    lane = lax.broadcasted_iota(jnp.int32, (1, wide), 1)
    lane_head = head_of(lane, heads)
    down = lax.broadcasted_iota(jnp.int32, (HEAD_DIM, wide), 0)
    over = lax.broadcasted_iota(jnp.int32, (HEAD_DIM, wide), 1)
    over_head = head_of(over, heads)
    spread = jnp.where((over - HEAD_DIM * over_head == down) & (over_head < heads), 1.0, 0.0).astype(BF16)

    def gain_row(block, which):
        gain = gains[block, which:which + 1, :]
        first = gain.astype(BF16)
        rest = gain - first.astype(F32)
        return lax.dot_general(first, spread, NN, preferred_element_type=F32) + split_dot(rest, spread)

    if wide > held:
        wq[:, :, held:, :] = jnp.zeros((2, 3, wide - held, depth), BF16)
        wo[:, held:, :] = jnp.zeros((2, wide - held, depth), BF16)
    inputs[3].wait()
    inputs[4].wait()
    gain_rows = [[gain_row(block, c) for c in range(2)] for block in range(2)]

    def modulated(block, xg):
        shift, gain = mod[0, block:block + 1], 1.0 + mod[1, block:block + 1]
        values = jnp.concatenate([xg[frame].astype(F32) for frame in range(frames)], axis=0)
        center = jnp.mean(values, axis=-1, keepdims=True)
        values = values - center
        spread_ = jnp.mean(values * values, axis=-1, keepdims=True)
        return (values * lax.rsqrt(spread_ + EPS) * gain + shift).astype(BF16)

    def projections(block, hmod):
        raw = lax.dot_general(
            hmod, wq[block].reshape(3 * wide, depth), NT, preferred_element_type=F32)
        count = raw.shape[0]
        two = jnp.concatenate([raw[:, :wide], raw[:, wide:2 * wide]], axis=0)
        square = split_dot(two * two, group) * (1.0 / HEAD_DIM)
        two = two * lax.rsqrt(square + EPS)
        return [two[:count] * gain_rows[block][0], two[count:] * gain_rows[block][1], raw[:, 2 * wide:]]

    def heads_out(block, half, attn):
        count = parts[half][1]
        product = lax.dot_general(
            jnp.concatenate(attn, axis=0).astype(BF16), wo[block], NN, preferred_element_type=F32)
        for frame in range(frames):
            partial[block][half][frame] = product[frame * count:(frame + 1) * count].astype(BF16)

    def sum_start(block, half):
        phase = block * n_part + half
        part, inbox = partial[block][half], rp[block][half]
        for j in list(range(1, n_chip)) + [0]:
            to = other_chip(j)
            started(remote(part.at[to * 2 + 1 - core], inbox.at[to], rs_send_p.at[phase, j], rs_recv_p.at[phase, to],
                           {"tm": partner}))

    def sum_arrived(phase, inbox, to):
        remote(inbox.at[to], inbox.at[to], rs_send_p.at[phase, 0], rs_recv_p.at[phase, to],
               {"tm": partner}).wait_recv()

    def sum_across(block, half):
        phase = block * n_part + half
        part, inbox, outbox = partial[block][half], rp[block][half], sx[block][half]
        for j in range(1, n_chip):
            to = other_chip(j)
            sum_arrived(phase, inbox, to)
            outbox[j - 1] = (part[to * 2 + core].astype(F32) + inbox[to].astype(F32)).astype(BF16)
            started(remote(outbox.at[j - 1], rx[block][half].at[j - 1], rs_send_x.at[phase, j - 1],
                           rs_recv_x.at[phase, j - 1], {"tm": to * 2 + core}))

    def all_across(half):
        part, inbox, outbox = partial[0][half], rp[0][half], chip_sum[half]
        for j in range(n_chip):
            to = other_chip(j)
            sum_arrived(half, inbox, to)
            outbox[to] = (part[to * 2 + core].astype(F32) + inbox[to].astype(F32)).astype(BF16)
        for j in range(1, n_chip):
            started(remote(outbox, all_sum[half].at[j - 1], rs_send_x.at[half, j - 1],
                           rs_recv_x.at[half, j - 1], {"tm": other_chip(j) * 2 + core}))

    def middle(half):
        first_row, count = parts[half]
        for j in range(1, n_chip):
            remote(chip_sum[half], all_sum[half].at[j - 1], rs_send_x.at[half, j - 1],
                   rs_recv_x.at[half, j - 1], {"tm": partner}).wait_recv()
        for c in range(n_chip):
            frame = c * 2 + core
            total = chip_sum[half][c].astype(F32)
            for j in range(1, n_chip):
                total = total + all_sum[half][j - 1, c].astype(F32)
            mine = xg0[frame].astype(F32)[first_row:first_row + count]
            xg1[half][frame] = (mine + mod[2, 0:1] * total).astype(BF16)
            started(remote(xg1[half].at[frame], xg1[half].at[frame], ag_send_p.at[1 + half, c],
                           ag_recv.at[1 + half, frame], {"tm": partner}))

    def sum_finish(block, half):
        phase = block * n_part + half
        sum_arrived(phase, rp[block][half], chip)
        total = partial[block][half][t].astype(F32) + rp[block][half][chip].astype(F32)
        for j in range(1, n_chip):
            remote(sx[block][half].at[j - 1], rx[block][half].at[j - 1], rs_send_x.at[phase, j - 1],
                   rs_recv_x.at[phase, j - 1], {"tm": partner}).wait_recv()
            total = total + rx[block][half][j - 1].astype(F32)
        return total

    gather_forward(0, xg0)
    if n_line > 1:
        relay(1, 0, True)
        relay_end(0, True)
    gather_finish(0, xg0)
    hmod = modulated(0, xg0)
    if n_line > 1:
        relay(1, 1, True)
        relay_end(1, True)
    for load in loads[:3]:
        load.wait()
    query, keys, values = projections(0, hmod)
    if n_line > 2:
        relay(2, 0, True)
    acc[...] = jnp.zeros_like(acc)
    for frame in range(frames):
        place(0, frame, keys[frame * rows:(frame + 1) * rows])
        place(1, frame, values[frame * rows:(frame + 1) * rows])
        _, offset = window(frame)
        for half, (first_row, count) in enumerate(parts):
            start = frame * rows + first_row
            some = query[start:start + count]
            some = jnp.concatenate([jnp.where(lane_head == head, some, 0.0) for head in range(heads)], axis=0)
            if offset:
                some = pltpu.roll(some, offset, 1)
            qbd[half][frame] = some.astype(BF16)
    pack(buf.at[b, a])
    for step in range(2, n_line):
        for cut in range(2):
            if (step, cut) != (2, 0):
                relay(step, cut, True)
        if step == 2:
            relay_across(True)
    relay_far(True)

    spot = lax.broadcasted_iota(jnp.int32, (1, n_line * rows + n_line * tail), 1)
    in_main = spot < n_line * main
    in_tail = lax.rem(spot, 2 * tail) < tail
    if n_line * main % (2 * tail):
        in_tail = lax.rem(jnp.maximum(spot - n_line * main, 0), 2 * tail) < tail

    def column_attention(halves, some, side):
        scores, values = [], []
        for frame in some:
            low, _ = window(frame)
            rest = buf[side, :, 2 * main:, low:low + wide].reshape(n_line * 2 * tail, wide)
            keys = buf[side, :, 0:main, low:low + wide].reshape(n_line * main, wide)
            value = buf[side, :, main:2 * main, low:low + wide].reshape(n_line * main, wide)
            keys = jnp.concatenate([keys, rest], axis=0)
            values.append(jnp.concatenate([value, rest], axis=0))
            query = jnp.concatenate([qbd[half][frame] for half in halves], axis=0)
            scores.append(lax.dot_general(query, keys, NT, preferred_element_type=F32))
        size = scores[0].shape[0]
        scores = jnp.concatenate(scores, axis=0)
        scores = jnp.where(in_main | in_tail, scores, -1e30)
        top = jnp.max(scores, axis=-1, keepdims=True)
        weights = jnp.exp((scores - top) * scale)
        norm = jnp.sum(weights, axis=-1, keepdims=True)
        moved = jnp.where(in_tail, 0.0, pltpu.roll(weights, tail, 1))
        weights = jnp.where(in_main, weights, moved)
        mixed = [
            lax.dot_general(weights[i * size:(i + 1) * size].astype(BF16), values[i], NN, preferred_element_type=F32)
            for i in range(len(some))]
        done = []
        for i, frame in enumerate(some):
            _, offset = window(frame)
            begin = 0
            for half in halves:
                count = parts[half][1]
                out = [jnp.zeros((count, wide), F32), jnp.zeros((count, wide), F32), jnp.ones((count, wide), F32)]
                for head in range(heads):
                    start = offset + head * HEAD_DIM
                    inside = (lane >= start) & (lane < start + HEAD_DIM)
                    here, there = slice(begin, begin + count), slice(i * size + begin, i * size + begin + count)
                    out = [jnp.where(inside, x, y)
                           for x, y in zip((mixed[i][here], top[there], norm[there]), out)]
                    begin += count
                done.append((half, frame, out))
        return done

    batches = [list(range(frames))[i:i + 4] for i in range(0, frames, 4)]
    for some in batches:
        for half, frame, out in column_attention(range(n_part), some, b):
            for i in range(3):
                early[half][i, frame] = out[i]
    for load in loads[3:]:
        load.wait()
    final_waits()

    def spatial(some, half):
        result = []
        for _, frame, (weighted, top, norm) in column_attention([half], some, 1 - b):
            before, top_before, norm_before = [early[half][i, frame] for i in range(3)]
            highest = jnp.maximum(top, top_before)
            now, then = jnp.exp((top - highest) * scale), jnp.exp((top_before - highest) * scale)
            total = (weighted * now + before * then) / (norm * now + norm_before * then)
            _, offset = window(frame)
            result.append(pltpu.roll(total, wide - offset, 1) if offset else total)
        return result

    def temporal(half, query, keys, values):
        count = parts[half][1]
        query, keys, values = [x.astype(BF16).astype(F32) for x in (query, keys, values)]
        out = []
        some = max(1, 16 // frames)
        for begin in range(0, frames, some):
            ones = [query[f * count:(f + 1) * count] for f in range(begin, min(begin + some, frames))]
            products = jnp.concatenate(
                [one * keys[g * count:(g + 1) * count] for one in ones for g in range(frames)], axis=0)
            products = split_dot(products, group) * scale
            for i in range(len(ones)):
                scores = [products[(i * frames + g) * count:(i * frames + g + 1) * count] for g in range(frames)]
                top = functools.reduce(jnp.maximum, scores)
                scores = [jnp.exp(score - top) for score in scores]
                norm = 1.0 / functools.reduce(jnp.add, scores)
                total = jnp.zeros((count, wide), F32)
                for g in range(frames):
                    weight = (scores[g] * norm).astype(BF16).astype(F32)
                    total = total + weight * values[g * count:(g + 1) * count]
                out.append(total)
        return out

    def finish(half):
        return xg1[half][t].astype(F32) + mod[2, 1:2] * sum_finish(1, half)

    for half in range(n_part):
        attn = []
        for some in batches:
            attn += spatial(some, half)
        if half:
            all_across(half - 1)
        heads_out(0, half, attn)
        sum_start(0, half)
    middle(0)
    all_across(n_part - 1)
    for half in range(n_part):
        gather_finish(1 + half, xg1[half])
        hmod = modulated(1, xg1[half])
        if half + 1 < n_part:
            middle(half + 1)
        triple = projections(1, hmod)
        if half:
            sum_across(1, half - 1)
        heads_out(1, half, temporal(half, *triple))
        sum_start(1, half)
    sum_across(1, n_part - 1)
    result = [finish(half) for half in range(n_part)]
    out_ref[0] = jnp.concatenate(result, axis=0).astype(BF16)

    for copy in pending:
        copy.wait_send()
    for step in range(n_line):
        for cut in range(2):
            relay(step, cut, False)
    for cut in range(2):
        relay_end(cut, False)
    relay_across(False)
    relay_far(False)


def local(n_tm, n_patch, stream, stale_keys, stale_values, modulation, w_qkv, w_out, qk_gain):
    frames, rows, width = stale_keys.shape
    depth = stream.shape[2]
    extra = -width % 16
    if extra:
        w_qkv = jnp.pad(w_qkv, ((0, 0), (0, 0), (0, extra), (0, 0)))
        w_out = jnp.pad(w_out, ((0, 0), (0, extra), (0, 0)))
    wide = max((frame * width % 128 + width + 127) // 128 * 128 for frame in range(frames))
    heads = width // HEAD_DIM
    n_chip, n_line = n_tm // 2, n_patch // 2
    cut = (rows // 2 + 15) // 16 * 16
    parts = ((0, cut), (cut, rows - cut))
    n_part = len(parts)
    vmem = pl.BlockSpec(memory_space=pltpu.VMEM)
    hbm = pl.BlockSpec(memory_space=pltpu.HBM)
    far = max(n_chip - 1, 1)

    def each(*lead):
        return [pltpu.VMEM((*lead, count, depth), BF16) for _, count in parts]

    dma = pltpu.SemaphoreType.DMA
    return pl.pallas_call(
        functools.partial(kernel, n_tm, n_patch, width, wide, parts),
        out_shape=jax.ShapeDtypeStruct(stream.shape, BF16),
        in_specs=[hbm] * 7,
        out_specs=vmem,
        scratch_shapes=[
            pltpu.VMEM((2, 3, wide, depth), BF16),
            pltpu.VMEM((2, wide, depth), BF16),
            pltpu.VMEM((2, frames, rows, width), BF16),
            pltpu.VMEM((3, 2, depth), F32),
            pltpu.VMEM((2, 2, HEAD_DIM), F32),
            pltpu.VMEM((2 * rows, frames * width), BF16),
            pltpu.VMEM((2, n_line, 2 * rows, frames * width), BF16),
            pltpu.VMEM((2, rows, wide), F32),
            pltpu.VMEM((2, rows, frames * width), F32),
            pltpu.VMEM((frames, rows, depth), BF16),
            *each(frames),
            *each(n_chip),
            *each(far, n_chip),
            *[pltpu.VMEM((frames, heads * count, wide), BF16) for _, count in parts],
            *[pltpu.VMEM((3, frames, count, wide), F32) for _, count in parts],
            *each(frames), *each(frames),
            *each(n_chip), *each(n_chip),
            *each(far), *each(far),
            *each(far), *each(far),
            dma((8,)),
            dma((5,)),
            dma((5, max(n_line, 2), 2)),
            dma((2, n_line, 2)),
            dma((1 + n_part, n_chip)),
            dma((1 + n_part, n_chip)),
            dma((1 + n_part, n_tm)),
            dma((2 * n_part, n_chip)),
            dma((2 * n_part, n_chip)),
            dma((2 * n_part, far)),
            dma((2 * n_part, far)),
        ],
        compiler_params=pltpu.CompilerParams(
            collective_id=0, has_side_effects=True, vmem_limit_bytes=56 * 1024 * 1024),
        cost_estimate=pl.CostEstimate(flops=4_000_000_000, bytes_accessed=8_000_000, transcendentals=1_000_000),
    )(stream, stale_keys, stale_values, jnp.transpose(modulation, (1, 0, 2)), w_qkv, w_out, qk_gain)


def solution(mesh):
    placed = (
        P("tm", "patch", None),
        P(None, "patch", "tm"),
        P(None, "patch", "tm"),
        P(),
        P(None, None, "tm", None),
        P(None, "tm", None),
        P(),
    )
    return jax.shard_map(
        functools.partial(local, mesh.shape["tm"], mesh.shape["patch"]),
        mesh=mesh, in_specs=placed, out_specs=P("tm", "patch", None), check_vma=False,
    )
```

```python
import functools

import jax
import jax.numpy as jnp
from jax import lax
from jax.experimental import pallas as pl
from jax.experimental.pallas import tpu as pltpu
from jax.sharding import PartitionSpec as P

HEAD_DIM = 72
EPS = 1e-06
MESH = pl.DeviceIdType.MESH
F32 = jnp.float32
BF16 = jnp.bfloat16
NT = (((1,), (1,)), ((), ()))
NN = (((1,), (0,)), ((), ()))


def head_of(index, heads):
    total = jnp.zeros_like(index)
    for head in range(1, heads + 1):
        total = total + jnp.where(index >= head * HEAD_DIM, 1, 0)
    return total


def split_dot(left, right):
    high = left.astype(BF16)
    low = (left - high.astype(F32)).astype(BF16)
    count = left.shape[0]
    if count % 16 == 0:
        both = lax.dot_general(jnp.concatenate([high, low], axis=0), right, NN, preferred_element_type=F32)
        return both[:count] + both[count:]
    return lax.dot_general(high, right, NN, preferred_element_type=F32) + lax.dot_general(
        low, right, NN, preferred_element_type=F32
    )


def kernel(
    n_tm, n_patch, width, wide, parts,
    stream_ref, old_k_ref, old_v_ref, mod_ref, w_qkv_ref, w_out_ref, gain_ref,
    out_ref,
    wq, wo, old, mod, gains, own, buf, stage, acc, xg0, *rest_refs,
):
    n_part = len(parts)
    rest_refs = list(rest_refs)

    def take():
        return [rest_refs.pop(0) for _ in range(n_part)]

    xg1, chip_sum, all_sum, qbd, early = take(), take(), take(), take(), take()
    partial = [take(), take()]
    rp, sx, rx = [take(), take()], [take(), take()], [take(), take()]
    (w_sem, in_sem, kv_send, kv_recv, ag_send_x, ag_send_p, ag_recv,
     rs_send_p, rs_recv_p, rs_send_x, rs_recv_x) = rest_refs
    frames, rows = old_k_ref.shape[0], old_k_ref.shape[1]
    depth = stream_ref.shape[2]
    heads = width // HEAD_DIM
    held = w_out_ref.shape[1]
    packed = frames * width
    main = rows // 16 * 16
    tail = rows - main
    n_chip = n_tm // 2
    n_line = n_patch // 2
    upper = rows // 16 * 16
    cuts = ((0, upper), (upper, 2 * rows - upper))
    scale = HEAD_DIM ** (-0.5)

    t = lax.axis_index("tm")
    chip, core = lax.div(t, 2), lax.rem(t, 2)
    partner = chip * 2 + 1 - core
    p = lax.axis_index("patch")
    a, b = lax.div(p, 2), lax.rem(p, 2)
    beside = a * 2 + 1 - b

    def other_chip(j):
        return lax.rem(chip + j, n_chip)

    inputs = [
        pltpu.make_async_copy(old_k_ref, old.at[0], in_sem.at[0]),
        pltpu.make_async_copy(old_v_ref, old.at[1], in_sem.at[1]),
        pltpu.make_async_copy(stream_ref.at[0], xg0.at[t], in_sem.at[2]),
        pltpu.make_async_copy(mod_ref, mod, in_sem.at[3]),
        pltpu.make_async_copy(gain_ref, gains, in_sem.at[4]),
    ]
    loads = []
    for block in range(2):
        for c in range(3):
            loads.append(pltpu.make_async_copy(
                w_qkv_ref.at[block, c], wq.at[block, c, pl.ds(0, held)], w_sem.at[block * 4 + c]))
        loads.append(pltpu.make_async_copy(
            w_out_ref.at[block], wo.at[block, pl.ds(0, held)], w_sem.at[block * 4 + 3]))
    for load in inputs + loads:
        load.start()

    barrier = pltpu.get_barrier_semaphore()

    def greet(**where):
        pl.semaphore_signal(barrier, inc=1, device_id=where, device_id_type=MESH)

    greet(tm=partner)
    greet(patch=beside)
    for j in range(1, n_chip):
        greet(tm=other_chip(j) * 2 + core)

    @pl.when(a > 0)
    def _():
        greet(patch=p - 2)

    @pl.when(a < n_line - 1)
    def _():
        greet(patch=p + 2)

    def window(frame):
        low = min(frame * width // 128 * 128, packed - wide)
        return low, frame * width - low

    def pack(slot):
        keys, values = acc[0], acc[1]
        slot[...] = jnp.concatenate(
            [keys[:main], values[:main], keys[main:], values[main:]], axis=0).astype(BF16)

    def place(which, frame, value):
        low, offset = window(frame)
        if offset:
            value = pltpu.roll(value, offset, 1)
        acc[which, :, low:low + wide] += value

    def stale(which):
        inputs[which].wait()
        for frame in range(frames):
            stage[which, :, 0:width] = old[which, frame].astype(F32)
            place(which, frame, stage[which])

    acc[...] = jnp.zeros_like(acc)
    stage[...] = jnp.zeros_like(stage)
    stale(0)
    own[0:main] = acc[0, 0:main].astype(BF16)

    met = 1 + n_chip + jnp.where(a > 0, 1, 0) + jnp.where(a < n_line - 1, 1, 0)
    pl.semaphore_wait(barrier, met)

    def remote(src, dst, send, recv, where):
        return pltpu.make_async_remote_copy(
            src_ref=src, dst_ref=dst, send_sem=send, recv_sem=recv, device_id=where, device_id_type=MESH)

    pending = []

    def started(copy):
        copy.start()
        pending.append(copy)

    def kv_copy(src, line, side, cut, kind, step, **where):
        first, count = cuts[cut]
        rows_of = pl.ds(first, count)
        return remote(src.at[rows_of], buf.at[side, line, rows_of], kv_send.at[kind, step, cut],
                      kv_recv.at[side, line, cut], where)

    def kv_arrived(line, side, cut):
        kv_copy(own, line, side, cut, 0, 0, patch=beside).wait_recv()

    def move(copy, go):
        copy.start() if go else copy.wait_send()

    def spot_on_line(line):
        return jnp.clip(line, 0, n_line - 1)

    even = n_line == 4
    at_end = (a == 0) | (a == n_line - 1)
    inward = jnp.where(a == 0, 1, a - 1)
    outward = jnp.where(a == 1, 0, n_line - 1)
    far_end = jnp.where(a == 1, n_line - 1, 0)

    def relay(step, cut, go):
        for kind, sign in ((0, 1), (1, -1)):
            origin = a - sign * step
            onward = a + sign
            line = spot_on_line(origin)
            src = buf.at[b, line] if step else own
            here = (origin >= 0) & (origin < n_line)

            if step:
                @pl.when(here)
                def _():
                    if go:
                        kv_arrived(line, b, cut)

                across = here
                if even and step == 1:
                    across = here & (origin != 0) & (origin != n_line - 1)
                if even and step == 2:
                    across = here & at_end
                if even and step == n_line - 1 and cut == 1:
                    across = None
                if across is not None:
                    @pl.when(across)
                    def _():
                        move(kv_copy(src, line, b, cut, 2 + kind, step, patch=beside), go)

            @pl.when(here & (onward >= 0) & (onward < n_line))
            def _():
                move(kv_copy(src, line, b, cut, kind, step, patch=spot_on_line(onward) * 2 + b), go)
        if step == 0:
            move(kv_copy(own, a, b, cut, 2, 0, patch=beside), go)

    def relay_across(go):
        if even:
            @pl.when(jnp.logical_not(at_end))
            def _():
                for cut in (1, 0):
                    move(kv_copy(buf.at[b, far_end], far_end, b, cut, 2, 2, patch=beside), go)

    def relay_end(cut, go):
        if even:
            @pl.when(at_end)
            def _():
                if go:
                    kv_arrived(a, 1 - b, cut)
                move(kv_copy(buf.at[1 - b, a], a, 1 - b, cut, 4, 0, patch=inward * 2 + b), go)

    def relay_far(go):
        if even:
            @pl.when(jnp.logical_not(at_end))
            def _():
                if go:
                    kv_arrived(far_end, 1 - b, 1)
                move(kv_copy(buf.at[1 - b, far_end], far_end, 1 - b, 1, 4, 1, patch=outward * 2 + b), go)

    def final_waits():
        for line in range(n_line):
            for cut in range(2):
                forwarded = False
                if even and line in (0, n_line - 1):
                    forwarded = at_end & (a == line)
                    if cut == 1:
                        forwarded = forwarded | (jnp.logical_not(at_end) & (far_end == line))

                if forwarded is False:
                    kv_arrived(line, 1 - b, cut)
                else:
                    @pl.when(jnp.logical_not(forwarded))
                    def _():
                        kv_arrived(line, 1 - b, cut)

    def gather_start(phase, src, xg):
        for j in range(1, n_chip):
            started(remote(src, xg.at[t], ag_send_x.at[phase, j], ag_recv.at[phase, t],
                           {"tm": other_chip(j) * 2 + core}))
        started(remote(src, xg.at[t], ag_send_p.at[phase, 0], ag_recv.at[phase, t], {"tm": partner}))

    def gather_arrived(phase, xg, frame):
        remote(xg.at[frame], xg.at[frame], ag_send_p.at[phase, 0], ag_recv.at[phase, frame],
               {"tm": partner}).wait_recv()

    def gather_forward(phase, xg):
        for j in range(1, n_chip):
            frame = other_chip(j) * 2 + core
            gather_arrived(phase, xg, frame)
            started(remote(xg.at[frame], xg.at[frame], ag_send_p.at[phase, j], ag_recv.at[phase, frame],
                           {"tm": partner}))

    def gather_finish(phase, xg):
        for j in range(n_chip):
            gather_arrived(phase, xg, other_chip(j) * 2 + 1 - core)

    relay(0, 0, True)
    inputs[2].wait()
    gather_start(0, xg0.at[t], xg0)
    stale(1)
    own[main:] = jnp.concatenate([acc[1, 0:main], acc[0, main:], acc[1, main:]], axis=0).astype(BF16)
    relay(0, 1, True)

    features = lax.broadcasted_iota(jnp.int32, (wide, wide), 0)
    columns = lax.broadcasted_iota(jnp.int32, (wide, wide), 1)
    same_head = (head_of(features, heads) == head_of(columns, heads)) & (features < width) & (columns < width)
    group = jnp.where(same_head, 1.0, 0.0).astype(BF16)
    lane = lax.broadcasted_iota(jnp.int32, (1, wide), 1)
    lane_head = head_of(lane, heads)
    down = lax.broadcasted_iota(jnp.int32, (HEAD_DIM, wide), 0)
    over = lax.broadcasted_iota(jnp.int32, (HEAD_DIM, wide), 1)
    over_head = head_of(over, heads)
    spread = jnp.where((over - HEAD_DIM * over_head == down) & (over_head < heads), 1.0, 0.0).astype(BF16)

    def gain_row(block, which):
        gain = gains[block, which:which + 1, :]
        first = gain.astype(BF16)
        rest = gain - first.astype(F32)
        return lax.dot_general(first, spread, NN, preferred_element_type=F32) + split_dot(rest, spread)

    if wide > held:
        wq[:, :, held:, :] = jnp.zeros((2, 3, wide - held, depth), BF16)
        wo[:, held:, :] = jnp.zeros((2, wide - held, depth), BF16)
    inputs[3].wait()
    inputs[4].wait()
    gain_rows = [[gain_row(block, c) for c in range(2)] for block in range(2)]

    def modulated(block, xg):
        shift, gain = mod[0, block:block + 1], 1.0 + mod[1, block:block + 1]
        values = jnp.concatenate([xg[frame].astype(F32) for frame in range(frames)], axis=0)
        center = jnp.mean(values, axis=-1, keepdims=True)
        values = values - center
        spread_ = jnp.mean(values * values, axis=-1, keepdims=True)
        return (values * lax.rsqrt(spread_ + EPS) * gain + shift).astype(BF16)

    def projections(block, hmod):
        raw = lax.dot_general(
            hmod, wq[block].reshape(3 * wide, depth), NT, preferred_element_type=F32)
        count = raw.shape[0]
        two = jnp.concatenate([raw[:, :wide], raw[:, wide:2 * wide]], axis=0)
        square = split_dot(two * two, group) * (1.0 / HEAD_DIM)
        two = two * lax.rsqrt(square + EPS)
        return [two[:count] * gain_rows[block][0], two[count:] * gain_rows[block][1], raw[:, 2 * wide:]]

    def heads_out(block, half, attn):
        count = parts[half][1]
        product = lax.dot_general(
            jnp.concatenate(attn, axis=0).astype(BF16), wo[block], NN, preferred_element_type=F32)
        for frame in range(frames):
            partial[block][half][frame] = product[frame * count:(frame + 1) * count].astype(BF16)

    def sum_start(block, half):
        phase = block * n_part + half
        part, inbox = partial[block][half], rp[block][half]
        for j in list(range(1, n_chip)) + [0]:
            to = other_chip(j)
            started(remote(part.at[to * 2 + 1 - core], inbox.at[to], rs_send_p.at[phase, j], rs_recv_p.at[phase, to],
                           {"tm": partner}))

    def sum_arrived(phase, inbox, to):
        remote(inbox.at[to], inbox.at[to], rs_send_p.at[phase, 0], rs_recv_p.at[phase, to],
               {"tm": partner}).wait_recv()

    def sum_across(block, half):
        phase = block * n_part + half
        part, inbox, outbox = partial[block][half], rp[block][half], sx[block][half]
        for j in range(1, n_chip):
            to = other_chip(j)
            sum_arrived(phase, inbox, to)
            outbox[j - 1] = (part[to * 2 + core].astype(F32) + inbox[to].astype(F32)).astype(BF16)
            started(remote(outbox.at[j - 1], rx[block][half].at[j - 1], rs_send_x.at[phase, j - 1],
                           rs_recv_x.at[phase, j - 1], {"tm": to * 2 + core}))

    def all_across(half):
        part, inbox, outbox = partial[0][half], rp[0][half], chip_sum[half]
        for j in range(n_chip):
            to = other_chip(j)
            sum_arrived(half, inbox, to)
            outbox[to] = (part[to * 2 + core].astype(F32) + inbox[to].astype(F32)).astype(BF16)
        for j in range(1, n_chip):
            started(remote(outbox, all_sum[half].at[j - 1], rs_send_x.at[half, j - 1],
                           rs_recv_x.at[half, j - 1], {"tm": other_chip(j) * 2 + core}))

    def middle(half):
        first_row, count = parts[half]
        for j in range(1, n_chip):
            remote(chip_sum[half], all_sum[half].at[j - 1], rs_send_x.at[half, j - 1],
                   rs_recv_x.at[half, j - 1], {"tm": partner}).wait_recv()
        for c in range(n_chip):
            frame = c * 2 + core
            total = chip_sum[half][c].astype(F32)
            for j in range(1, n_chip):
                total = total + all_sum[half][j - 1, c].astype(F32)
            mine = xg0[frame].astype(F32)[first_row:first_row + count]
            xg1[half][frame] = (mine + mod[2, 0:1] * total).astype(BF16)
            started(remote(xg1[half].at[frame], xg1[half].at[frame], ag_send_p.at[1 + half, c],
                           ag_recv.at[1 + half, frame], {"tm": partner}))

    def sum_finish(block, half):
        phase = block * n_part + half
        sum_arrived(phase, rp[block][half], chip)
        total = partial[block][half][t].astype(F32) + rp[block][half][chip].astype(F32)
        for j in range(1, n_chip):
            remote(sx[block][half].at[j - 1], rx[block][half].at[j - 1], rs_send_x.at[phase, j - 1],
                   rs_recv_x.at[phase, j - 1], {"tm": partner}).wait_recv()
            total = total + rx[block][half][j - 1].astype(F32)
        return total

    gather_forward(0, xg0)
    if n_line > 1:
        relay(1, 0, True)
        relay_end(0, True)
    gather_finish(0, xg0)
    hmod = modulated(0, xg0)
    if n_line > 1:
        relay(1, 1, True)
        relay_end(1, True)
    for load in loads[:3]:
        load.wait()
    query, keys, values = projections(0, hmod)
    if n_line > 2:
        relay(2, 0, True)
    acc[...] = jnp.zeros_like(acc)
    for frame in range(frames):
        place(0, frame, keys[frame * rows:(frame + 1) * rows])
        place(1, frame, values[frame * rows:(frame + 1) * rows])
        _, offset = window(frame)
        for half, (first_row, count) in enumerate(parts):
            start = frame * rows + first_row
            some = query[start:start + count]
            some = jnp.concatenate([jnp.where(lane_head == head, some, 0.0) for head in range(heads)], axis=0)
            if offset:
                some = pltpu.roll(some, offset, 1)
            qbd[half][frame] = some.astype(BF16)
    pack(buf.at[b, a])
    for step in range(2, n_line):
        for cut in range(2):
            if (step, cut) != (2, 0):
                relay(step, cut, True)
        if step == 2:
            relay_across(True)
    relay_far(True)

    spot = lax.broadcasted_iota(jnp.int32, (1, n_line * rows + n_line * tail), 1)
    in_main = spot < n_line * main
    in_tail = lax.rem(spot, 2 * tail) < tail
    if n_line * main % (2 * tail):
        in_tail = lax.rem(jnp.maximum(spot - n_line * main, 0), 2 * tail) < tail

    def column_attention(halves, some, side):
        scores, values = [], []
        for frame in some:
            low, _ = window(frame)
            rest = buf[side, :, 2 * main:, low:low + wide].reshape(n_line * 2 * tail, wide)
            keys = buf[side, :, 0:main, low:low + wide].reshape(n_line * main, wide)
            value = buf[side, :, main:2 * main, low:low + wide].reshape(n_line * main, wide)
            keys = jnp.concatenate([keys, rest], axis=0)
            values.append(jnp.concatenate([value, rest], axis=0))
            query = jnp.concatenate([qbd[half][frame] for half in halves], axis=0)
            scores.append(lax.dot_general(query, keys, NT, preferred_element_type=F32))
        size = scores[0].shape[0]
        scores = jnp.concatenate(scores, axis=0)
        scores = jnp.where(in_main | in_tail, scores, -1e30)
        top = jnp.max(scores, axis=-1, keepdims=True)
        weights = jnp.exp((scores - top) * scale)
        norm = jnp.sum(weights, axis=-1, keepdims=True)
        moved = jnp.where(in_tail, 0.0, pltpu.roll(weights, tail, 1))
        weights = jnp.where(in_main, weights, moved)
        mixed = [
            lax.dot_general(weights[i * size:(i + 1) * size].astype(BF16), values[i], NN, preferred_element_type=F32)
            for i in range(len(some))]
        done = []
        for i, frame in enumerate(some):
            _, offset = window(frame)
            begin = 0
            for half in halves:
                count = parts[half][1]
                out = [jnp.zeros((count, wide), F32), jnp.zeros((count, wide), F32), jnp.ones((count, wide), F32)]
                for head in range(heads):
                    start = offset + head * HEAD_DIM
                    inside = (lane >= start) & (lane < start + HEAD_DIM)
                    here, there = slice(begin, begin + count), slice(i * size + begin, i * size + begin + count)
                    out = [jnp.where(inside, x, y)
                           for x, y in zip((mixed[i][here], top[there], norm[there]), out)]
                    begin += count
                done.append((half, frame, out))
        return done

    batches = [list(range(frames))[i:i + 4] for i in range(0, frames, 4)]
    for some in batches:
        for half, frame, out in column_attention(range(n_part), some, b):
            for i in range(3):
                early[half][i, frame] = out[i]
    for load in loads[3:]:
        load.wait()
    final_waits()

    def spatial(some, half):
        result = []
        for _, frame, (weighted, top, norm) in column_attention([half], some, 1 - b):
            before, top_before, norm_before = [early[half][i, frame] for i in range(3)]
            highest = jnp.maximum(top, top_before)
            now, then = jnp.exp((top - highest) * scale), jnp.exp((top_before - highest) * scale)
            total = (weighted * now + before * then) / (norm * now + norm_before * then)
            _, offset = window(frame)
            result.append(pltpu.roll(total, wide - offset, 1) if offset else total)
        return result

    def temporal(half, query, keys, values):
        count = parts[half][1]
        query, keys, values = [x.astype(BF16).astype(F32) for x in (query, keys, values)]
        out = []
        some = max(1, 16 // frames)
        for begin in range(0, frames, some):
            ones = [query[f * count:(f + 1) * count] for f in range(begin, min(begin + some, frames))]
            products = jnp.concatenate(
                [one * keys[g * count:(g + 1) * count] for one in ones for g in range(frames)], axis=0)
            products = split_dot(products, group) * scale
            for i in range(len(ones)):
                scores = [products[(i * frames + g) * count:(i * frames + g + 1) * count] for g in range(frames)]
                top = functools.reduce(jnp.maximum, scores)
                scores = [jnp.exp(score - top) for score in scores]
                norm = 1.0 / functools.reduce(jnp.add, scores)
                total = jnp.zeros((count, wide), F32)
                for g in range(frames):
                    weight = (scores[g] * norm).astype(BF16).astype(F32)
                    total = total + weight * values[g * count:(g + 1) * count]
                out.append(total)
        return out

    def finish(half):
        return xg1[half][t].astype(F32) + mod[2, 1:2] * sum_finish(1, half)

    for half in range(n_part):
        attn = []
        for some in batches:
            attn += spatial(some, half)
        if half:
            all_across(half - 1)
        heads_out(0, half, attn)
        sum_start(0, half)
    middle(0)
    all_across(n_part - 1)
    for half in range(n_part):
        gather_finish(1 + half, xg1[half])
        hmod = modulated(1, xg1[half])
        if half + 1 < n_part:
            middle(half + 1)
        triple = projections(1, hmod)
        if half:
            sum_across(1, half - 1)
        heads_out(1, half, temporal(half, *triple))
        sum_start(1, half)
    sum_across(1, n_part - 1)
    result = [finish(half) for half in range(n_part)]
    out_ref[0] = jnp.concatenate(result, axis=0)

    for copy in pending:
        copy.wait_send()
    for step in range(n_line):
        for cut in range(2):
            relay(step, cut, False)
    for cut in range(2):
        relay_end(cut, False)
    relay_across(False)
    relay_far(False)


def local(n_tm, n_patch, stream, stale_keys, stale_values, modulation, w_qkv, w_out, qk_gain):
    frames, rows, width = stale_keys.shape
    depth = stream.shape[2]
    extra = -width % 16
    if extra:
        w_qkv = jnp.pad(w_qkv, ((0, 0), (0, 0), (0, extra), (0, 0)))
        w_out = jnp.pad(w_out, ((0, 0), (0, extra), (0, 0)))
    wide = max((frame * width % 128 + width + 127) // 128 * 128 for frame in range(frames))
    heads = width // HEAD_DIM
    n_chip, n_line = n_tm // 2, n_patch // 2
    cut = (rows // 2 + 15) // 16 * 16
    parts = ((0, cut), (cut, rows - cut))
    n_part = len(parts)
    vmem = pl.BlockSpec(memory_space=pltpu.VMEM)
    hbm = pl.BlockSpec(memory_space=pltpu.HBM)
    far = max(n_chip - 1, 1)

    def each(*lead):
        return [pltpu.VMEM((*lead, count, depth), BF16) for _, count in parts]

    dma = pltpu.SemaphoreType.DMA
    return pl.pallas_call(
        functools.partial(kernel, n_tm, n_patch, width, wide, parts),
        out_shape=jax.ShapeDtypeStruct(stream.shape, F32),
        in_specs=[hbm] * 7,
        out_specs=vmem,
        scratch_shapes=[
            pltpu.VMEM((2, 3, wide, depth), BF16),
            pltpu.VMEM((2, wide, depth), BF16),
            pltpu.VMEM((2, frames, rows, width), BF16),
            pltpu.VMEM((3, 2, depth), F32),
            pltpu.VMEM((2, 2, HEAD_DIM), F32),
            pltpu.VMEM((2 * rows, frames * width), BF16),
            pltpu.VMEM((2, n_line, 2 * rows, frames * width), BF16),
            pltpu.VMEM((2, rows, wide), F32),
            pltpu.VMEM((2, rows, frames * width), F32),
            pltpu.VMEM((frames, rows, depth), BF16),
            *each(frames),
            *each(n_chip),
            *each(far, n_chip),
            *[pltpu.VMEM((frames, heads * count, wide), BF16) for _, count in parts],
            *[pltpu.VMEM((3, frames, count, wide), F32) for _, count in parts],
            *each(frames), *each(frames),
            *each(n_chip), *each(n_chip),
            *each(far), *each(far),
            *each(far), *each(far),
            dma((8,)),
            dma((5,)),
            dma((5, max(n_line, 2), 2)),
            dma((2, n_line, 2)),
            dma((1 + n_part, n_chip)),
            dma((1 + n_part, n_chip)),
            dma((1 + n_part, n_tm)),
            dma((2 * n_part, n_chip)),
            dma((2 * n_part, n_chip)),
            dma((2 * n_part, far)),
            dma((2 * n_part, far)),
        ],
        compiler_params=pltpu.CompilerParams(
            collective_id=0, has_side_effects=True, vmem_limit_bytes=56 * 1024 * 1024),
        cost_estimate=pl.CostEstimate(flops=4_000_000_000, bytes_accessed=8_000_000, transcendentals=1_000_000),
    )(stream, stale_keys, stale_values, jnp.transpose(modulation, (1, 0, 2)), w_qkv, w_out, qk_gain).astype(BF16)


def solution(mesh):
    placed = (
        P("tm", "patch", None),
        P(None, "patch", "tm"),
        P(None, "patch", "tm"),
        P(),
        P(None, None, "tm", None),
        P(None, "tm", None),
        P(),
    )
    return jax.shard_map(
        functools.partial(local, mesh.shape["tm"], mesh.shape["patch"]),
        mesh=mesh, in_specs=placed, out_specs=P("tm", "patch", None), check_vma=False,
    )
```
